512 devices in a mesh: prow: 16 (over z, core), pcol: 32 (over x, y).
Axes of the slice: x: 4, y: 8, z: 8, core: 2. Of those that a mesh axis runs over, the one named last changes fastest.
Arguments:
- window: float32 [8192, 32768], P('prow', 'pcol'), may hold values from -6 to 6
- panel: float32 [8192, 256], P(('prow', 'pcol')), may hold values from -0.375 to 0.375
- linv: float32 [256, 256], replicated, as said below
- pivots: int32 [256], replicated, may hold values from 0 to 8191, as said below
Outputs:
- updated: float32 [8192, 32768], P('prow', 'pcol')
The draws below stay inside these ranges and needn't reach their ends.
Inputs may be any that keep to these rules, and one draw needn't show every extreme that they name: `pivots`: each entry k is either k itself or a row at or past 256; entries of the second kind are all distinct. `linv`: zero above the diagonal, ones on it.
All inputs are finite; a program needn't handle non-finite values.
Results may differ from the reference program's by a relative error of at most 0.000055.
Values sent between devices are 32-bit elements; how exact they have to be, the bound alone decides.
No kernel may reach another device: no remote copies, remote signals or barrier semaphores. Data moves between devices by JAX's collectives and lax.ppermute only.
A program may use at most 64 MiB of HBM per device.

```python
import math
import jax
import jax.numpy as jnp
from jax import lax

NB = 256
ROWS_DEV = 512
ROWS = 8192
COLS = 32768


def draw_linv(key, part):
    key = jax.random.fold_in(key, 5)
    values = jax.random.normal(key, (NB, NB), jnp.float32)
    lower = jnp.tril(values, -1) / math.sqrt(NB)
    return lower + jnp.eye(NB, dtype=jnp.float32)


def draw_pivots(key, part):
    key = jax.random.fold_in(key, 11)
    key_bias, key_score, key_order, key_stay = jax.random.split(key, 4)
    bias = jax.random.randint(key_bias, (ROWS // ROWS_DEV,), 0, 4)
    rowid = jnp.arange(ROWS, dtype=jnp.int32)
    score = jax.random.randint(key_score, (ROWS,), 0, 4096) + bias[rowid // ROWS_DEV] * 4096
    score = jnp.where(rowid < NB, -1, score)
    forced_row = (rowid % ROWS_DEV == ROWS_DEV - 1) & (rowid >= NB)
    score = jnp.where(forced_row, 20000, score)
    chosen = jnp.argsort(-score, stable=True)[:NB].astype(jnp.int32)
    order = jax.random.permutation(key_order, NB)
    chosen = chosen[order]
    ident = jnp.arange(NB, dtype=jnp.int32)
    forced = (chosen % ROWS_DEV == ROWS_DEV - 1) & (chosen >= NB)
    stay = ((jax.random.randint(key_stay, (NB,), 0, 5) == 0) | (ident == 0)) & jnp.logical_not(forced)
    return jnp.where(stay, ident, chosen).astype(jnp.int32)


def block_levels(key, shape, cuts, least, largest):
    def one(axis_at, shards_of):
        draws = jax.random.uniform(jax.random.fold_in(jax.random.fold_in(key, 6), axis_at), (shards_of,), jnp.float32, least / len(cuts), largest / len(cuts))
        return jnp.repeat(jnp.exp(draws), shape[axis_at] // shards_of).reshape((-1,) + (1,) * (len(shape) - axis_at - 1))

    factor_of = one(*cuts[0])
    for cut in cuts[1:]:
        factor_of = factor_of * one(*cut)
    return factor_of


def centred(key, extent, scale, bound, cuts=(), kind=jnp.bfloat16):
    values = scale * jax.random.normal(key, extent, jnp.float32)
    if cuts:
        values = values * block_levels(key, extent, cuts, -0.22, 0.18)
    return jnp.clip(values, -bound, bound).astype(kind)


def setup_inputs(seed: int = 0) -> dict:
    splits = jax.random.split(jax.random.key(seed), 5)
    return {
        "window": centred(splits[0], (ROWS, COLS), 1.0, 6.0, ((0, 16), (1, 32)), jnp.float32),
        "panel": centred(splits[1], (ROWS, NB), NB ** -0.5, 0.375, ((0, 512),), jnp.float32),
        "linv": draw_linv(jax.random.fold_in(splits[4], 71), 0),
        "pivots": draw_pivots(jax.random.fold_in(splits[4], 71), 0),
    }


def reference(window, panel, linv, pivots):
    ident = jnp.arange(NB, dtype=jnp.int32)
    moved = pivots != ident
    top = window[pivots]
    solved = jnp.dot(linv, top, precision=lax.Precision.HIGHEST, preferred_element_type=jnp.float32)
    target = jnp.where(moved, pivots, ROWS).astype(jnp.int32)
    swapped = window.at[ident].set(top)
    swapped = swapped.at[target].set(window[:NB], mode="drop")
    updated = swapped - jnp.dot(panel, solved, precision=lax.Precision.HIGHEST, preferred_element_type=jnp.float32)
    return updated.at[:NB].set(solved)
```

```python
import functools

import jax
import jax.numpy as jnp
from jax import lax
from jax.experimental import pallas as pl
from jax.experimental.pallas import tpu as pltpu
from jax.sharding import PartitionSpec as P

CORES = 2
YS = 8
LANES = 128
PARAMS = pltpu.CompilerParams(vmem_limit_bytes=32 * 1024 * 1024)


def vmem(count):
    return [pl.BlockSpec(memory_space=pltpu.VMEM)] * count


def smem(count):
    return [pl.BlockSpec(memory_space=pltpu.SMEM)] * count


def cost(flops, nbytes):
    return pl.CostEstimate(flops=flops, bytes_accessed=nbytes, transcendentals=0)


def pick_kernel(piv, me, win, own, give, owned, count):
    nrows = win.shape[0]
    half = own.shape[0]
    first = me[0] * nrows
    base = lax.rem(me[0], CORES) * half
    other = half - base

    def place(k):
        local = piv[k] - first
        inside = (local >= 0) & (local < nrows)
        return inside, jnp.where(inside, local, k)

    def listed(k, total):
        inside, _ = place(k)
        owned[total] = k
        moved = inside & (piv[k] != k)
        return total + moved.astype(jnp.int32)

    def step(i, total):
        _, source = place(other + i)
        give[pl.ds(i, 1), :] = win[pl.ds(source, 1), :]
        _, source = place(base + i)
        own[pl.ds(i, 1), :] = win[pl.ds(source, 1), :]
        total = listed(2 * i, total)
        return listed(2 * i + 1, total)

    count[0] = lax.fori_loop(0, half, step, jnp.int32(0), unroll=4)


def pick(pivots, me, window, half):
    ncols = window.shape[1]
    block = jax.ShapeDtypeStruct((half, ncols), window.dtype)
    return pl.pallas_call(
        pick_kernel,
        out_shape=(
            block,
            block,
            jax.ShapeDtypeStruct((2 * half + 8,), jnp.int32),
            jax.ShapeDtypeStruct((1,), jnp.int32),
        ),
        in_specs=smem(2) + vmem(1),
        out_specs=tuple(vmem(2) + smem(2)),
        compiler_params=PARAMS,
        cost_estimate=cost(0, 16 * half * ncols),
        name="pick",
    )(pivots, me, window)


def tiles(ncols):
    return [slice(c, c + LANES) for c in range(0, ncols, LANES)]


def deal_kernel(me, owner, own, got, *refs):
    lines, (out, strip) = refs[:-2], refs[-2:]
    half, ncols = own.shape
    core = lax.rem(me[0], CORES)
    partner = me[0] + 1 - 2 * core
    who = owner[pl.ds(pl.multiple_of(core * half, half), half), :]
    first = jnp.where(me[0] == 0, 1, 0)
    theirs = jnp.where(first == 1, (who == partner).astype(jnp.int32), (who != me[0]).astype(jnp.int32)) == 1
    for cols in tiles(ncols):
        out[:, cols] = jnp.where(theirs, got[:, cols], own[:, cols])
    place(me[2], lines, strip)


def place(index, pieces, out):
    rows = pieces[0].shape[0]
    for d, piece in enumerate(pieces):
        source = lax.rem(index - d + len(pieces), len(pieces))
        out[pl.ds(pl.multiple_of(source * rows, rows), rows), :] = piece[...]


def deal(me, owner, own, got, lines):
    half, ncols = own.shape
    rows, nb = lines[0].shape
    return pl.pallas_call(
        deal_kernel,
        out_shape=(
            jax.ShapeDtypeStruct(own.shape, own.dtype),
            jax.ShapeDtypeStruct((rows * len(lines), nb), own.dtype),
        ),
        in_specs=smem(1) + vmem(3 + len(lines)),
        out_specs=tuple(vmem(2)),
        compiler_params=PARAMS,
        cost_estimate=cost(0, 12 * half * ncols),
        name="deal",
    )(me, owner, own, got, *lines)


def home_kernel(nz, me, owner, got, *refs):
    strips, outs, panel = refs[: -nz - 1], refs[-nz - 1 : -1], refs[-1]
    part, ncols = outs[0].shape
    core = lax.rem(me[0], CORES)
    z = me[0] // CORES
    at = pl.multiple_of(core * (part * nz) + z * part, part)
    chip = owner[pl.ds(at, part), :] // CORES
    for cols in tiles(ncols):
        former = got[0:part, cols]
        top = former
        for source in range(1, nz):
            top = jnp.where(chip == source, got[source * part : (source + 1) * part, cols], top)
        for d in range(nz):
            outs[d][:, cols] = jnp.where(chip == lax.rem(z + d, nz), former, top)
    place(me[1], strips, panel)


def home(nz, me, owner, got, strips):
    half, ncols = got.shape
    rows, nb = strips[0].shape
    chunk = jax.ShapeDtypeStruct((half // nz, ncols), got.dtype)
    out = pl.pallas_call(
        functools.partial(home_kernel, nz),
        out_shape=(chunk,) * nz + (jax.ShapeDtypeStruct((rows * len(strips), nb), got.dtype),),
        in_specs=smem(1) + vmem(2 + len(strips)),
        out_specs=tuple(vmem(nz + 1)),
        compiler_params=PARAMS,
        cost_estimate=cost(0, 8 * half * ncols),
        name="home",
    )(me, owner, got, *strips)
    return out[:nz], out[nz]


def pair_kernel(nz, me, owner, own, *refs):
    pieces, out = refs[:nz], refs[nz]
    half, ncols = own.shape
    part = half // nz
    core = lax.rem(me[0], CORES)
    z = me[0] // CORES
    partner = me[0] + 1 - 2 * core
    mate = jnp.where(me[0] == 0, partner, me[0])
    for d in range(nz):
        at = pl.multiple_of(lax.rem(z - d + nz, nz) * part, part)
        who = owner[pl.ds(pl.multiple_of(core * half + at, part), part), :]
        mine = (who == me[0]) | (who == mate)
        for cols in tiles(ncols):
            out[pl.ds(at, part), cols] = jnp.where(mine, own[pl.ds(at, part), cols], pieces[d][:, cols])


def pair(nz, me, owner, own, pieces):
    half, ncols = own.shape
    return pl.pallas_call(
        functools.partial(pair_kernel, nz),
        out_shape=jax.ShapeDtypeStruct(own.shape, own.dtype),
        in_specs=smem(1) + vmem(2 + nz),
        out_specs=pl.BlockSpec(memory_space=pltpu.VMEM),
        compiler_params=PARAMS,
        cost_estimate=cost(0, 12 * half * ncols),
        name="pair",
    )(me, owner, own, *pieces)


def ready_kernel(nz, me, owner, own, got, *refs):
    pieces = refs[:nz]
    top, former = refs[nz:]
    half, ncols = own.shape
    part = half // nz
    core = lax.rem(me[0], CORES)
    z = me[0] // CORES
    partner = me[0] + 1 - 2 * core
    for d in range(nz):
        at = pl.multiple_of(lax.rem(z - d + nz, nz) * part, part)
        who = owner[pl.ds(pl.multiple_of(core * half + at, part), part), :]
        here = who == me[0]
        there = who == partner
        for cols in tiles(ncols):
            mine = own[pl.ds(at, part), cols]
            theirs = got[pl.ds(at, part), cols]
            far = pieces[d][:, cols]
            top[pl.ds(at, part), cols] = jnp.where(here, mine, jnp.where(there, theirs, far))
            former[pl.ds(at, part), cols] = jnp.where(me[0] == 1, theirs, far)


def ready(nz, me, owner, own, got, pieces):
    half, ncols = own.shape
    block = jax.ShapeDtypeStruct(own.shape, own.dtype)
    return pl.pallas_call(
        functools.partial(ready_kernel, nz),
        out_shape=(block, block),
        in_specs=smem(1) + vmem(3 + nz),
        out_specs=tuple(vmem(2)),
        compiler_params=PARAMS,
        cost_estimate=cost(0, 20 * half * ncols),
        name="ready",
    )(me, owner, own, got, *pieces)


def final_kernel(me, piv, owned, count, owner, linv, panel, win, top, former, give, got, out, full, old):
    nrows = win.shape[0]
    half = top.shape[0]
    nb = 2 * half
    first = me[0] * nrows
    core = lax.rem(me[0], CORES)
    base = pl.multiple_of(core * half, half)
    other = pl.multiple_of(half - base, half)
    who = owner[pl.ds(other, half), :]
    full[pl.ds(base, half), :] = top[...]
    old[pl.ds(base, half), :] = former[...]
    old[pl.ds(other, half), :] = got[...]
    for cols in tiles(win.shape[1]):
        full[pl.ds(other, half), cols] = jnp.where(who == me[0], give[:, cols], got[:, cols])
    out[...] = win[...]

    @pl.when(me[0] == 0)
    def _():
        old[...] = win[0:nb, :]

    def put(i, carry):
        k = owned[i]
        row = piv[k] - first
        out[pl.ds(row, 1), :] = old[pl.ds(k, 1), :]
        return carry

    lax.fori_loop(0, count[0], put, 0)
    solved = jnp.dot(
        linv[...], full[...], precision=lax.Precision.HIGHEST, preferred_element_type=jnp.float32
    )
    out[...] = out[...] - jnp.dot(
        panel[...], solved, precision=lax.Precision.HIGHEST, preferred_element_type=jnp.float32
    )

    @pl.when(me[0] == 0)
    def _():
        out[0:nb, :] = solved


def final(me, pivots, owned, count, owner, linv, panel, window, top, former, give, got):
    nrows, ncols = window.shape
    half = top.shape[0]
    nb = 2 * half
    step = min(256, ncols)
    whole = lambda shape: pl.BlockSpec(shape, lambda c: (0, 0))
    strip = lambda rows: pl.BlockSpec((rows, step), lambda c: (0, c))
    return pl.pallas_call(
        final_kernel,
        grid=(ncols // step,),
        out_shape=jax.ShapeDtypeStruct(window.shape, window.dtype),
        in_specs=smem(4)
        + [whole(owner.shape), whole(linv.shape), whole(panel.shape)]
        + [strip(nrows)]
        + [strip(half)] * 4,
        out_specs=strip(nrows),
        scratch_shapes=[pltpu.VMEM((nb, step), jnp.float32), pltpu.VMEM((nb, step), jnp.float32)],
        compiler_params=PARAMS,
        cost_estimate=cost(12 * (nb + nrows) * nb * ncols, 8 * nrows * ncols),
        name="final",
    )(me, pivots, owned, count, owner, linv, panel, window, top, former, give, got)


def on_device(nprow, npcol, window, panel, linv, pivots):
    nrows, ncols = window.shape
    nbw = pivots.shape[0]
    half = nbw // CORES
    nz = nprow // CORES
    ny = min(YS, npcol)
    columns = [[z * CORES + core for z in range(nz)] for core in range(CORES)]

    def moved(value, axis, pairs):
        return value if pairs[0] == (0, 0) else lax.ppermute(value, axis, pairs)

    def swap(value):
        return moved(value, "prow", [(p, p ^ 1) for p in range(nprow)])

    def along_z(value, d):
        return moved(value, "prow", [(p, (p + CORES * d) % nprow) for p in range(nprow)])

    def along_x(value, d):
        return moved(value, "pcol", [(c, (c + ny * d) % npcol) for c in range(npcol)])

    def along_y(value, d):
        return moved(value, "pcol", [(c, c // ny * ny + (c + d) % ny) for c in range(npcol)])

    pcol = lax.axis_index("pcol")
    me = jnp.stack([lax.axis_index("prow"), pcol // ny, pcol % ny]).astype(jnp.int32)
    owner = jnp.broadcast_to((pivots // nrows)[:, None], (nbw, LANES))

    lines = [along_y(panel, d) for d in range(ny)]
    own, give, owned, count = pick(pivots, me, window, half)
    got = swap(give)
    chip, strip = deal(me, owner, own, got, lines)
    strips = [along_x(strip, d) for d in range(npcol // ny)]
    dealt = lax.all_to_all(chip, "prow", 0, 0, axis_index_groups=columns, tiled=True)
    chunks, whole = home(nz, me, owner, dealt, strips)
    pieces = [along_z(chunks[d], d) for d in range(nz)]
    last = swap(pair(nz, me, owner, own, pieces))
    top, former = ready(nz, me, owner, own, got, pieces)
    return final(me, pivots, owned, count, owner, linv, whole, window, top, former, give, last)


def solution(mesh):
    return jax.shard_map(
        functools.partial(on_device, mesh.shape["prow"], mesh.shape["pcol"]),
        mesh=mesh,
        in_specs=(P("prow", "pcol"), P(("prow", "pcol"), None), P(), P()),
        out_specs=P("prow", "pcol"),
        check_vma=False,
    )
```

```python
import functools

import jax
import jax.numpy as jnp
from jax import lax
from jax.experimental import pallas as pl
from jax.experimental.pallas import tpu as pltpu
from jax.sharding import PartitionSpec as P

CORES = 2
LANES = 128
STEP = 256
PARAMS = pltpu.CompilerParams(vmem_limit_bytes=32 * 1024 * 1024)


def vmem(count):
    return [pl.BlockSpec(memory_space=pltpu.VMEM)] * count


def smem(count):
    return [pl.BlockSpec(memory_space=pltpu.SMEM)] * count


def cost(flops, nbytes):
    return pl.CostEstimate(flops=flops, bytes_accessed=nbytes, transcendentals=0)


def tiles(ncols):
    return [slice(c, c + LANES) for c in range(0, ncols, LANES)]


def sides(me, half):
    core = lax.rem(me, CORES)
    return core, me + 1 - 2 * core, core * half, half - core * half


def scan_kernel(nrows, piv, me, lists, counts):
    half = piv.shape[0] // CORES
    _, _, base, other = sides(me[0], half)
    first = me[0] * nrows

    def step(i, totals):
        new = []
        for side, start in enumerate((base, other)):
            local = piv[start + i] - first
            inside = (local >= 0) & (local < nrows)
            lists[side, totals[side]] = start + i
            new.append(totals[side] + inside.astype(jnp.int32))
        return tuple(new)

    counts[0], counts[1] = lax.fori_loop(0, half, step, (jnp.int32(0), jnp.int32(0)), unroll=8)


def scan(nrows, pivots, me):
    half = pivots.shape[0] // CORES
    return pl.pallas_call(
        functools.partial(scan_kernel, nrows),
        out_shape=(
            jax.ShapeDtypeStruct((CORES, half), jnp.int32),
            jax.ShapeDtypeStruct((CORES,), jnp.int32),
        ),
        in_specs=smem(2),
        out_specs=tuple(smem(2)),
        compiler_params=PARAMS,
        cost_estimate=cost(0, 2**20),
        name="scan",
    )(pivots, me)


def pick_kernel(piv, me, lists, counts, win, own, give):
    nrows = win.shape[0]
    half = own.shape[0]
    _, _, base, other = sides(me[0], half)
    first = me[0] * nrows
    for side, start, out in ((1, other, give), (0, base, own)):
        out[...] = win[pl.ds(pl.multiple_of(start, half), half), :]

        def put(i, carry, side=side, start=start, out=out):
            k = lists[side, i]
            out[pl.ds(k - start, 1), :] = win[pl.ds(piv[k] - first, 1), :]
            return carry

        lax.fori_loop(0, counts[side], put, 0)


def pick(pivots, me, lists, counts, window):
    half = pivots.shape[0] // CORES
    ncols = window.shape[1]
    block = jax.ShapeDtypeStruct((half, ncols), window.dtype)
    return pl.pallas_call(
        pick_kernel,
        out_shape=(block, block),
        in_specs=smem(4) + vmem(1),
        out_specs=tuple(vmem(2)),
        compiler_params=PARAMS,
        cost_estimate=cost(0, 16 * half * ncols),
        name="pick",
    )(pivots, me, lists, counts, window)


def half_of(owner, base, half):
    return owner[pl.ds(pl.multiple_of(base, half), half), :]


def deal_kernel(me, owner, own, got, out):
    half, ncols = own.shape
    _, partner, base, _ = sides(me[0], half)
    who = half_of(owner, base, half)
    theirs = (who == partner) | ((who != me[0]) & (who != jnp.where(me[0] == 0, who, -1)))
    for cols in tiles(ncols):
        out[:, cols] = jnp.where(theirs, got[:, cols], own[:, cols])


def pair_kernel(me, owner, own, got, left, out):
    half, ncols = own.shape
    _, partner, base, _ = sides(me[0], half)
    who = half_of(owner, base, half)
    mine = (who == me[0]) | (who == jnp.where(me[0] == 0, partner, me[0]))
    for cols in tiles(ncols):
        out[:, cols] = jnp.where(mine, own[:, cols], got[:, cols])


def home_kernel(nz, me, owner, got, out):
    half, ncols = got.shape
    part = half // nz
    _, _, base, _ = sides(me[0], half)
    at = pl.multiple_of(base + me[0] // CORES * part, part)
    chip = owner[pl.ds(at, part), :] // CORES
    for cols in tiles(ncols):
        former = got[0:part, cols]
        top = former
        for z in range(1, nz):
            top = jnp.where(chip == z, got[z * part : (z + 1) * part, cols], top)
        for z in range(nz):
            out[z * part : (z + 1) * part, cols] = jnp.where(chip == z, former, top)


def choose(kernel, name, me, owner, *blocks):
    shape = blocks[0].shape
    return pl.pallas_call(
        kernel,
        out_shape=jax.ShapeDtypeStruct(shape, blocks[0].dtype),
        in_specs=smem(1) + vmem(1 + len(blocks)),
        out_specs=pl.BlockSpec(memory_space=pltpu.VMEM),
        compiler_params=PARAMS,
        cost_estimate=cost(0, 12 * shape[0] * shape[1]),
        name=name,
    )(me, owner, *blocks)


def parts(value):
    high = value.astype(jnp.bfloat16)
    return high, (value - high.astype(jnp.float32)).astype(jnp.bfloat16)


def split_kernel(linv, panel, left, right):
    for source, out in ((linv, left), (panel, right)):
        nb = source.shape[1]
        high, low = parts(source[...])
        out[:, 0:nb] = high
        out[:, nb : 2 * nb] = low
        out[:, 2 * nb : 3 * nb] = high


def split(linv, panel):
    shapes = [jax.ShapeDtypeStruct((a.shape[0], 3 * a.shape[1]), jnp.bfloat16) for a in (linv, panel)]
    return pl.pallas_call(
        split_kernel,
        out_shape=tuple(shapes),
        in_specs=vmem(2),
        out_specs=tuple(vmem(2)),
        compiler_params=PARAMS,
        cost_estimate=cost(0, 10 * (linv.size + panel.size)),
        name="split",
    )(linv, panel)


def ready_kernel(piv, me, lists, counts, owner, own, got, far, win, top, swapped):
    half, ncols = own.shape
    nrows = win.shape[0]
    _, partner, base, _ = sides(me[0], half)
    first = me[0] * nrows
    who = half_of(owner, base, half)
    for cols in tiles(ncols):
        theirs = jnp.where(who == partner, got[:, cols], far[:, cols])
        top[:, cols] = jnp.where(who == me[0], own[:, cols], theirs)
    swapped[...] = win[...]

    def put(source, side, start):
        def one(i, carry):
            k = lists[side, i]
            swapped[pl.ds(piv[k] - first, 1), :] = source[pl.ds(k - start, 1), :]
            return carry

        lax.fori_loop(0, counts[side], one, 0)

    @pl.when(me[0] == 0)
    def _():
        put(win, 0, 0)
        put(win, 1, 0)

    @pl.when(me[0] == 1)
    def _():
        put(got, 0, base)

    @pl.when(me[0] > 1)
    def _():
        put(far, 0, base)


def ready(pivots, me, lists, counts, owner, own, got, far, window):
    return pl.pallas_call(
        ready_kernel,
        out_shape=(
            jax.ShapeDtypeStruct(own.shape, own.dtype),
            jax.ShapeDtypeStruct(window.shape, window.dtype),
        ),
        in_specs=smem(4) + vmem(5),
        out_specs=tuple(vmem(2)),
        compiler_params=PARAMS,
        cost_estimate=cost(0, 8 * window.size + 16 * own.size),
        name="ready",
    )(pivots, me, lists, counts, owner, own, got, far, window)


def final_kernel(piv, me, lists, counts, owner, left, right, swapped, top, give, got, out, full, rhs):
    half = top.shape[0]
    nb = 2 * half
    nrows, step = out.shape
    first = me[0] * nrows
    _, _, base, other = sides(me[0], half)
    base = pl.multiple_of(base, half)
    other = pl.multiple_of(other, half)
    at = pl.multiple_of(pl.program_id(0) * step, step)
    who = half_of(owner, other, half)
    full[pl.ds(base, half), :] = top[:, pl.ds(at, step)]
    for c in range(0, step, LANES):
        cols = pl.ds(pl.multiple_of(at + c, LANES), LANES)
        full[pl.ds(other, half), c : c + LANES] = jnp.where(who == me[0], give[:, cols], got[:, cols])

    def product(rows, value):
        high, low = parts(value)
        rhs[0:nb, :] = high
        rhs[nb : 2 * nb, :] = high
        rhs[2 * nb : 3 * nb, :] = low
        return jnp.dot(rows[...], rhs[...], preferred_element_type=jnp.float32)

    out[...] = swapped[:, pl.ds(at, step)]

    def put(i, carry):
        k = lists[1, i]
        out[pl.ds(piv[k] - first, 1), :] = got[pl.ds(k - other, 1), pl.ds(at, step)]
        return carry

    lax.fori_loop(0, jnp.where(me[0] == 0, 0, counts[1]), put, 0)
    solved = product(left, full[...])
    out[...] = out[...] - product(right, solved)

    @pl.when(me[0] == 0)
    def _():
        out[0:nb, :] = solved


def final(pivots, me, lists, counts, owner, left, right, swapped, top, give, got):
    nrows, ncols = swapped.shape
    nb = 2 * top.shape[0]
    step = min(STEP, ncols)
    return pl.pallas_call(
        final_kernel,
        grid=(ncols // step,),
        out_shape=jax.ShapeDtypeStruct(swapped.shape, swapped.dtype),
        in_specs=smem(4) + vmem(7),
        out_specs=pl.BlockSpec((nrows, step), lambda c: (0, c)),
        scratch_shapes=[pltpu.VMEM((nb, step), jnp.float32), pltpu.VMEM((3 * nb, step), jnp.bfloat16)],
        compiler_params=PARAMS,
        cost_estimate=cost(6 * (nb + nrows) * nb * ncols, 8 * nrows * ncols),
        name="final",
    )(pivots, me, lists, counts, owner, left, right, swapped, top, give, got)


def on_device(nprow, npcol, window, panel, linv, pivots):
    nrows, ncols = window.shape
    nbw = pivots.shape[0]
    nz = nprow // CORES
    columns = [[z * CORES + core for z in range(nz)] for core in range(CORES)]

    def swap(value):
        return lax.ppermute(value, "prow", [(p, p ^ 1) for p in range(nprow)])

    def exchange(value):
        return lax.all_to_all(value, "prow", 0, 0, axis_index_groups=columns, tiled=True)

    me = lax.axis_index("prow").astype(jnp.int32)[None]
    owner = jnp.broadcast_to((pivots // nrows)[:, None], (nbw, LANES))
    lists, counts = scan(nrows, pivots, me)
    own, give = pick(pivots, me, lists, counts, window)
    got = swap(give)
    dealt = exchange(choose(deal_kernel, "deal", me, owner, own, got))
    copies = jnp.broadcast_to(panel[None], (npcol,) + panel.shape)
    whole = lax.all_to_all(copies, "pcol", 0, 0).reshape(nrows, nbw)
    far = exchange(choose(functools.partial(home_kernel, nz), "home", me, owner, dealt))
    left, right = split(linv, whole)
    last = swap(choose(pair_kernel, "pair", me, owner, own, far, left))
    top, swapped = ready(pivots, me, lists, counts, owner, own, got, far, window)
    return final(pivots, me, lists, counts, owner, left, right, swapped, top, give, last)


def solution(mesh):
    return jax.shard_map(
        functools.partial(on_device, mesh.shape["prow"], mesh.shape["pcol"]),
        mesh=mesh,
        in_specs=(P("prow", "pcol"), P(("prow", "pcol"), None), P(), P()),
        out_specs=P("prow", "pcol"),
        check_vma=False,
    )
```

```python
import functools

import jax
import jax.numpy as jnp
from jax import lax
from jax.experimental import pallas as pl
from jax.experimental.pallas import tpu as pltpu
from jax.sharding import PartitionSpec as P

CORES = 2
YS = 8
LANES = 128
STEP = 256
PARAMS = pltpu.CompilerParams(vmem_limit_bytes=32 * 1024 * 1024)
ROOMY = pltpu.CompilerParams(vmem_limit_bytes=58 * 1024 * 1024)


def vmem(count):
    return [pl.BlockSpec(memory_space=pltpu.VMEM)] * count


def smem(count):
    return [pl.BlockSpec(memory_space=pltpu.SMEM)] * count


def cost(flops, nbytes):
    return pl.CostEstimate(flops=flops, bytes_accessed=nbytes, transcendentals=0)


def tiles(ncols):
    return [slice(c, c + LANES) for c in range(0, ncols, LANES)]


def sides(me, half):
    core = lax.rem(me, CORES)
    return core, me + 1 - 2 * core, core * half, half - core * half


def each(count, body):
    def four(j, carry):
        for u in range(4):
            body(jnp.minimum(4 * j + u, count - 1))
        return carry

    lax.fori_loop(0, (count + 3) // 4, four, 0)


def pick_kernel(piv, me, win, own, give, slots, rows, counts, held, sem):
    nrows = win.shape[0]
    half = own.shape[0]
    _, _, base, other = sides(me[0], half)
    first = me[0] * nrows
    load = pltpu.make_async_copy(win, held, sem)
    load.start()

    def step(i, totals):
        new = []
        for side, start in enumerate((base, other)):
            local = piv[start + i] - first
            inside = (local >= 0) & (local < nrows)
            slots[side, totals[side]] = i
            rows[side, totals[side]] = local
            new.append(totals[side] + inside.astype(jnp.int32))
        return tuple(new)

    totals = lax.fori_loop(0, half, step, (jnp.int32(0), jnp.int32(0)), unroll=8)
    load.wait()
    for side, start, out in ((1, other, give), (0, base, own)):
        counts[side] = totals[side]
        out[...] = held[pl.ds(pl.multiple_of(start, half), half), :]

        def put(i, side=side, out=out):
            out[pl.ds(slots[side, i], 1), :] = held[pl.ds(rows[side, i], 1), :]

        each(totals[side], put)


def pick(pivots, me, window):
    half = pivots.shape[0] // CORES
    ncols = window.shape[1]
    block = jax.ShapeDtypeStruct((half, ncols), window.dtype)
    table = jax.ShapeDtypeStruct((CORES, half), jnp.int32)
    out = pl.pallas_call(
        pick_kernel,
        out_shape=(block, block, table, table, jax.ShapeDtypeStruct((CORES,), jnp.int32)),
        in_specs=smem(2) + [pl.BlockSpec(memory_space=pltpu.HBM)],
        out_specs=tuple(vmem(2) + smem(3)),
        scratch_shapes=[pltpu.VMEM(window.shape, window.dtype), pltpu.SemaphoreType.DMA],
        compiler_params=ROOMY,
        cost_estimate=cost(0, 16 * half * ncols),
        name="pick",
    )(pivots, me, window)
    return out[0], out[1], out[2:]


def half_of(owner, base, half):
    return owner[pl.ds(pl.multiple_of(base, half), half), :]


def deal_kernel(me, owner, own, got, panel, out, same):
    half, ncols = own.shape
    _, partner, base, _ = sides(me[0], half)
    who = half_of(owner, base, half)
    theirs = (who == partner) | ((who != me[0]) & (who != jnp.where(me[0] == 0, who, -1)))
    for cols in tiles(ncols):
        out[:, cols] = jnp.where(theirs, got[:, cols], own[:, cols])
    same[...] = panel[...]


def line_kernel(me, *refs):
    pieces, out = refs[:-1], refs[-1]
    rows = pieces[0].shape[0]
    at = me[2] // 2
    for d, piece in enumerate(pieces):
        source = lax.rem(at - d + len(pieces), len(pieces))
        out[pl.ds(pl.multiple_of(source * rows, rows), rows), :] = piece[...]


def home_kernel(nz, part_rows, me, owner, got, mine, theirs, out, strip):
    half, ncols = got.shape
    part = half // nz
    _, _, base, _ = sides(me[0], half)
    at = pl.multiple_of(base + me[0] // CORES * part, part)
    chip = owner[pl.ds(at, part), :] // CORES
    for cols in tiles(ncols):
        former = got[0:part, cols]
        top = former
        for z in range(1, nz):
            top = jnp.where(chip == z, got[z * part : (z + 1) * part, cols], top)
        for z in range(nz):
            out[z * part : (z + 1) * part, cols] = jnp.where(chip == z, former, top)
    odd = lax.rem(me[2], 2)
    for q in range(mine.shape[0] // part_rows):
        source = slice(q * part_rows, (q + 1) * part_rows)
        for block, side in ((mine, odd), (theirs, 1 - odd)):
            strip[pl.ds(pl.multiple_of((2 * q + side) * part_rows, part_rows), part_rows), :] = block[source, :]


def pair_kernel(me, owner, own, got, token, out):
    half, ncols = own.shape
    _, partner, base, _ = sides(me[0], half)
    who = half_of(owner, base, half)
    mine = (who == me[0]) | (who == jnp.where(me[0] == 0, partner, me[0]))
    for cols in tiles(ncols):
        out[:, cols] = jnp.where(mine, own[:, cols], got[:, cols])


def local(kernel, name, shapes, me, *blocks):
    outs = tuple(jax.ShapeDtypeStruct(shape, jnp.float32) for shape in shapes)
    return pl.pallas_call(
        kernel,
        out_shape=outs,
        in_specs=smem(1) + vmem(len(blocks)),
        out_specs=tuple(vmem(len(outs))),
        compiler_params=PARAMS,
        cost_estimate=cost(0, 4 * sum(block.size for block in blocks)),
        name=name,
    )(me, *blocks)


def parts(value):
    high = value.astype(jnp.bfloat16)
    return high, (value - high.astype(jnp.float32)).astype(jnp.bfloat16)


def split_kernel(me, linv, *refs):
    strips, (left, right, token) = refs[:-3], refs[-3:]
    nb = linv.shape[1]

    def put(value, out, rows):
        high, low = parts(value)
        out[rows, 0:nb] = high
        out[rows, nb : 2 * nb] = low
        out[rows, 2 * nb : 3 * nb] = high

    put(linv[...], left, slice(None))
    count = strips[0].shape[0]
    for d, strip in enumerate(strips):
        source = lax.rem(me[1] - d + len(strips), len(strips))
        put(strip[...], right, pl.ds(pl.multiple_of(source * count, count), count))
    token[...] = jnp.zeros_like(token)


def split(me, linv, strips):
    nb = linv.shape[1]
    nrows = sum(strip.shape[0] for strip in strips)
    return pl.pallas_call(
        split_kernel,
        out_shape=(
            jax.ShapeDtypeStruct((nb, 3 * nb), jnp.bfloat16),
            jax.ShapeDtypeStruct((nrows, 3 * nb), jnp.bfloat16),
            jax.ShapeDtypeStruct((8, LANES), jnp.float32),
        ),
        in_specs=smem(1) + vmem(1 + len(strips)),
        out_specs=tuple(vmem(3)),
        compiler_params=PARAMS,
        cost_estimate=cost(0, 10 * nb * (nb + nrows)),
        name="split",
    )(me, linv, *strips)


def ready_kernel(me, slots, rows, counts, owner, own, got, far, win, top, swapped):
    half, ncols = own.shape
    _, partner, base, other = sides(me[0], half)
    who = half_of(owner, base, half)
    for cols in tiles(ncols):
        theirs = jnp.where(who == partner, got[:, cols], far[:, cols])
        top[:, cols] = jnp.where(who == me[0], own[:, cols], theirs)
    swapped[...] = win[...]

    def put(source, side, start):
        def one(i):
            swapped[pl.ds(rows[side, i], 1), :] = source[pl.ds(start + slots[side, i], 1), :]

        each(counts[side], one)

    @pl.when(me[0] == 0)
    def _():
        put(win, 0, base)
        put(win, 1, other)

    @pl.when(me[0] == 1)
    def _():
        put(got, 0, 0)

    @pl.when(me[0] > 1)
    def _():
        put(far, 0, 0)


def ready(me, table, owner, own, got, far, window):
    return pl.pallas_call(
        ready_kernel,
        out_shape=(
            jax.ShapeDtypeStruct(own.shape, own.dtype),
            jax.ShapeDtypeStruct(window.shape, window.dtype),
        ),
        in_specs=smem(4) + vmem(5),
        out_specs=tuple(vmem(2)),
        compiler_params=PARAMS,
        cost_estimate=cost(0, 8 * window.size + 16 * own.size),
        name="ready",
    )(me, *table, owner, own, got, far, window)


def final_kernel(me, slots, rows, counts, owner, left, right, swapped, top, give, got, out, full, rhs):
    half = top.shape[0]
    nb = 2 * half
    nrows, step = out.shape
    _, _, base, other = sides(me[0], half)
    base = pl.multiple_of(base, half)
    other = pl.multiple_of(other, half)
    at = pl.multiple_of(pl.program_id(0) * step, step)
    who = half_of(owner, other, half)
    full[pl.ds(base, half), :] = top[:, pl.ds(at, step)]
    for c in range(0, step, LANES):
        cols = pl.ds(pl.multiple_of(at + c, LANES), LANES)
        full[pl.ds(other, half), c : c + LANES] = jnp.where(who == me[0], give[:, cols], got[:, cols])

    def product(factor, value):
        high, low = parts(value)
        rhs[0:nb, :] = high
        rhs[nb : 2 * nb, :] = high
        rhs[2 * nb : 3 * nb, :] = low
        return jnp.dot(factor[...], rhs[...], preferred_element_type=jnp.float32)

    out[...] = swapped[:, pl.ds(at, step)]

    def put(i):
        out[pl.ds(rows[1, i], 1), :] = got[pl.ds(slots[1, i], 1), pl.ds(at, step)]

    each(jnp.where(me[0] == 0, 0, counts[1]), put)
    solved = product(left, full[...])
    out[...] = out[...] - product(right, solved)

    @pl.when(me[0] == 0)
    def _():
        out[0:nb, :] = solved


def final(me, table, owner, left, right, swapped, top, give, got):
    nrows, ncols = swapped.shape
    nb = 2 * top.shape[0]
    step = min(STEP, ncols)
    return pl.pallas_call(
        final_kernel,
        grid=(ncols // step,),
        out_shape=jax.ShapeDtypeStruct(swapped.shape, swapped.dtype),
        in_specs=smem(4) + vmem(7),
        out_specs=pl.BlockSpec((nrows, step), lambda c: (0, c)),
        scratch_shapes=[pltpu.VMEM((nb, step), jnp.float32), pltpu.VMEM((3 * nb, step), jnp.bfloat16)],
        compiler_params=PARAMS,
        cost_estimate=cost(6 * (nb + nrows) * nb * ncols, 8 * nrows * ncols),
        name="final",
    )(me, *table, owner, left, right, swapped, top, give, got)


def on_device(nprow, npcol, window, panel, linv, pivots):
    nrows, ncols = window.shape
    nbw = pivots.shape[0]
    nz = nprow // CORES
    columns = [[z * CORES + core for z in range(nz)] for core in range(CORES)]

    def swap(value):
        return lax.ppermute(value, "prow", [(p, p ^ 1) for p in range(nprow)])

    def exchange(value):
        return lax.all_to_all(value, "prow", 0, 0, axis_index_groups=columns, tiled=True)

    def ring(value, size, stride):
        span = size * stride
        pairs = lambda d: [(c, c // span * span + (c + d * stride) % span) for c in range(npcol)]
        return [value] + [lax.ppermute(value, "pcol", pairs(d)) for d in range(1, size)]

    pcol = lax.axis_index("pcol")
    me = jnp.stack([lax.axis_index("prow"), pcol // YS, pcol % YS]).astype(jnp.int32)
    owner = jnp.broadcast_to((pivots // nrows)[:, None], (nbw, LANES))
    half, strip = nbw // CORES, (YS * panel.shape[0], nbw)

    own, give, table = pick(pivots, me, window)
    got = swap(give)
    chip, rows = local(deal_kernel, "deal", [own.shape, panel.shape], me, owner, own, got, panel)
    dealt = exchange(chip)
    (mine,) = local(line_kernel, "line", [(strip[0] // 2, nbw)], me, *ring(rows, YS // 2, 2))
    theirs = lax.ppermute(mine, "pcol", [(c, c ^ 1) for c in range(npcol)])
    kernel = functools.partial(home_kernel, nz, panel.shape[0])
    chosen, whole = local(kernel, "home", [own.shape, strip], me, owner, dealt, mine, theirs)
    far = exchange(chosen)
    left, right, token = split(me, linv, ring(whole, npcol // YS, YS))
    (paired,) = local(pair_kernel, "pair", [own.shape], me, owner, own, far, token)
    last = swap(paired)
    top, swapped = ready(me, table, owner, own, got, far, window)
    return final(me, table, owner, left, right, swapped, top, give, last)


def solution(mesh):
    return jax.shard_map(
        functools.partial(on_device, mesh.shape["prow"], mesh.shape["pcol"]),
        mesh=mesh,
        in_specs=(P("prow", "pcol"), P(("prow", "pcol"), None), P(), P()),
        out_specs=P("prow", "pcol"),
        check_vma=False,
    )
```

```python
import functools

import jax
import jax.numpy as jnp
from jax import lax
from jax.experimental import pallas as pl
from jax.experimental.pallas import tpu as pltpu
from jax.sharding import PartitionSpec as P

CORES = 2
YS = 8
LANES = 128
STEP = 256
PARAMS = pltpu.CompilerParams(vmem_limit_bytes=32 * 1024 * 1024)
ROOMY = pltpu.CompilerParams(vmem_limit_bytes=58 * 1024 * 1024)


def vmem(count):
    return [pl.BlockSpec(memory_space=pltpu.VMEM)] * count


def smem(count):
    return [pl.BlockSpec(memory_space=pltpu.SMEM)] * count


def cost(flops, nbytes):
    return pl.CostEstimate(flops=flops, bytes_accessed=nbytes, transcendentals=0)


def tiles(ncols):
    return [slice(c, c + LANES) for c in range(0, ncols, LANES)]


def sides(half):
    me = lax.axis_index("prow")
    core = lax.rem(me, CORES)
    return me, me + 1 - 2 * core, core * half, half - core * half


def each(count, body):
    def four(j, carry):
        for u in range(4):
            body(jnp.minimum(4 * j + u, count - 1))
        return carry

    lax.fori_loop(0, (count + 3) // 4, four, 0)


def pick_kernel(piv, win, own, give, slots, rows, counts, held, sem):
    nrows = win.shape[0]
    half = own.shape[0]
    me, _, base, other = sides(half)
    first = me * nrows
    load = pltpu.make_async_copy(win, held, sem)
    load.start()

    def step(i, totals):
        new = []
        for side, start in enumerate((base, other)):
            local = piv[start + i] - first
            inside = (local >= 0) & (local < nrows)
            slots[side, totals[side]] = i
            rows[side, totals[side]] = local
            new.append(totals[side] + inside.astype(jnp.int32))
        return tuple(new)

    totals = lax.fori_loop(0, half, step, (jnp.int32(0), jnp.int32(0)), unroll=8)
    load.wait()
    for side, start, out in ((1, other, give), (0, base, own)):
        counts[side] = totals[side]
        out[...] = held[pl.ds(pl.multiple_of(start, half), half), :]

        def put(i, side=side, out=out):
            out[pl.ds(slots[side, i], 1), :] = held[pl.ds(rows[side, i], 1), :]

        each(totals[side], put)


def pick(pivots, window):
    half = pivots.shape[0] // CORES
    ncols = window.shape[1]
    block = jax.ShapeDtypeStruct((half, ncols), window.dtype)
    table = jax.ShapeDtypeStruct((CORES, half), jnp.int32)
    out = pl.pallas_call(
        pick_kernel,
        out_shape=(block, block, table, table, jax.ShapeDtypeStruct((CORES,), jnp.int32)),
        in_specs=smem(1) + [pl.BlockSpec(memory_space=pl.ANY)],
        out_specs=tuple(vmem(2) + smem(3)),
        scratch_shapes=[pltpu.VMEM(window.shape, window.dtype), pltpu.SemaphoreType.DMA],
        compiler_params=ROOMY,
        cost_estimate=cost(0, 16 * half * ncols),
        name="pick",
    )(pivots, window)
    return out[0], out[1], out[2:]


def half_of(owner, base, half):
    return owner[pl.ds(pl.multiple_of(base, half), half), :]


def deal_kernel(owner, own, got, panel, beside, out, rows):
    half, ncols = own.shape
    me, partner, base, _ = sides(half)
    who = half_of(owner, base, half)
    theirs = (who == partner) | ((who != me) & (who != jnp.where(me == 0, who, -1)))
    for cols in tiles(ncols):
        out[:, cols] = jnp.where(theirs, got[:, cols], own[:, cols])
    count = panel.shape[0]
    odd = lax.rem(lax.axis_index("pcol"), 2)
    rows[pl.ds(pl.multiple_of(odd * count, count), count), :] = panel[...]
    rows[pl.ds(pl.multiple_of((1 - odd) * count, count), count), :] = beside[...]


def ordered(index, pieces, put):
    count = pieces[0].shape[0]
    for d, piece in enumerate(pieces):
        source = lax.rem(index - d + len(pieces), len(pieces))
        put(pl.ds(pl.multiple_of(source * count, count), count), piece[...])


def home_kernel(nz, owner, got, *refs):
    pieces, (out, strip) = refs[:-2], refs[-2:]
    half, ncols = got.shape
    part = half // nz
    me, _, base, _ = sides(half)
    at = pl.multiple_of(base + me // CORES * part, part)
    chip = owner[pl.ds(at, part), :] // CORES
    for cols in tiles(ncols):
        former = got[0:part, cols]
        top = former
        for z in range(1, nz):
            top = jnp.where(chip == z, got[z * part : (z + 1) * part, cols], top)
        for z in range(nz):
            out[z * part : (z + 1) * part, cols] = jnp.where(chip == z, former, top)

    def put(rows, value):
        strip[rows, :] = value

    ordered(lax.rem(lax.axis_index("pcol"), YS) // 2, pieces, put)


def pair_kernel(owner, own, got, token, out):
    half, ncols = own.shape
    me, partner, base, _ = sides(half)
    who = half_of(owner, base, half)
    mine = (who == me) | (who == jnp.where(me == 0, partner, me))
    for cols in tiles(ncols):
        out[:, cols] = jnp.where(mine, own[:, cols], got[:, cols])


def local(kernel, name, params, shapes, *blocks):
    outs = tuple(jax.ShapeDtypeStruct(shape, jnp.float32) for shape in shapes)
    return pl.pallas_call(
        kernel,
        out_shape=outs,
        in_specs=vmem(len(blocks)),
        out_specs=tuple(vmem(len(outs))),
        compiler_params=params,
        cost_estimate=cost(0, 4 * sum(block.size for block in blocks)),
        name=name,
    )(*blocks)


def parts(value):
    high = value.astype(jnp.bfloat16)
    return high, (value - high.astype(jnp.float32)).astype(jnp.bfloat16)


def split_kernel(linv, *refs):
    strips, (left, right, token) = refs[:-3], refs[-3:]
    nb = linv.shape[1]

    def put(value, out, rows):
        high, low = parts(value)
        out[rows, 0:nb] = high
        out[rows, nb : 2 * nb] = low
        out[rows, 2 * nb : 3 * nb] = high

    put(linv[...], left, slice(None))
    ordered(lax.axis_index("pcol") // YS, strips, lambda rows, value: put(value, right, rows))
    token[...] = jnp.zeros_like(token)


def split(linv, strips):
    nb = linv.shape[1]
    nrows = sum(strip.shape[0] for strip in strips)
    return pl.pallas_call(
        split_kernel,
        out_shape=(
            jax.ShapeDtypeStruct((nb, 3 * nb), jnp.bfloat16),
            jax.ShapeDtypeStruct((nrows, 3 * nb), jnp.bfloat16),
            jax.ShapeDtypeStruct((8, LANES), jnp.float32),
        ),
        in_specs=vmem(1 + len(strips)),
        out_specs=tuple(vmem(3)),
        compiler_params=ROOMY,
        cost_estimate=cost(0, 10 * nb * (nb + nrows)),
        name="split",
    )(linv, *strips)


def ready_kernel(slots, rows, counts, owner, own, got, far, win, top, swapped):
    half, ncols = own.shape
    me, partner, base, other = sides(half)
    who = half_of(owner, base, half)
    for cols in tiles(ncols):
        theirs = jnp.where(who == partner, got[:, cols], far[:, cols])
        top[:, cols] = jnp.where(who == me, own[:, cols], theirs)
    swapped[...] = win[...]

    def put(source, side, start):
        def one(i):
            swapped[pl.ds(rows[side, i], 1), :] = source[pl.ds(start + slots[side, i], 1), :]

        each(counts[side], one)

    @pl.when(me == 0)
    def _():
        put(win, 0, base)
        put(win, 1, other)

    @pl.when(me == 1)
    def _():
        put(got, 0, 0)

    @pl.when(me > 1)
    def _():
        put(far, 0, 0)


def ready(table, owner, own, got, far, window):
    return pl.pallas_call(
        ready_kernel,
        out_shape=(
            jax.ShapeDtypeStruct(own.shape, own.dtype),
            jax.ShapeDtypeStruct(window.shape, window.dtype),
        ),
        in_specs=smem(3) + vmem(5),
        out_specs=tuple(vmem(2)),
        compiler_params=PARAMS,
        cost_estimate=cost(0, 8 * window.size + 16 * own.size),
        name="ready",
    )(*table, owner, own, got, far, window)


def final_kernel(slots, rows, counts, owner, left, right, swapped, top, give, got, out, full, rhs):
    half = top.shape[0]
    nb = 2 * half
    nrows, step = out.shape
    me, _, base, other = sides(half)
    base = pl.multiple_of(base, half)
    other = pl.multiple_of(other, half)
    at = pl.multiple_of(pl.program_id(0) * step, step)
    who = half_of(owner, other, half)
    full[pl.ds(base, half), :] = top[:, pl.ds(at, step)]
    for c in range(0, step, LANES):
        cols = pl.ds(pl.multiple_of(at + c, LANES), LANES)
        full[pl.ds(other, half), c : c + LANES] = jnp.where(who == me, give[:, cols], got[:, cols])

    def product(factor, value):
        high, low = parts(value)
        rhs[0:nb, :] = high
        rhs[nb : 2 * nb, :] = high
        rhs[2 * nb : 3 * nb, :] = low
        return jnp.dot(factor[...], rhs[...], preferred_element_type=jnp.float32)

    out[...] = swapped[:, pl.ds(at, step)]

    def put(i):
        out[pl.ds(rows[1, i], 1), :] = got[pl.ds(slots[1, i], 1), pl.ds(at, step)]

    each(jnp.where(me == 0, 0, counts[1]), put)
    solved = product(left, full[...])
    out[...] = out[...] - product(right, solved)

    @pl.when(me == 0)
    def _():
        out[0:nb, :] = solved


def final(table, owner, left, right, swapped, top, give, got):
    nrows, ncols = swapped.shape
    nb = 2 * top.shape[0]
    step = min(STEP, ncols)
    return pl.pallas_call(
        final_kernel,
        grid=(ncols // step,),
        out_shape=jax.ShapeDtypeStruct(swapped.shape, swapped.dtype),
        in_specs=smem(3) + vmem(7),
        out_specs=pl.BlockSpec((nrows, step), lambda c: (0, c)),
        scratch_shapes=[pltpu.VMEM((nb, step), jnp.float32), pltpu.VMEM((3 * nb, step), jnp.bfloat16)],
        compiler_params=PARAMS,
        cost_estimate=cost(6 * (nb + nrows) * nb * ncols, 8 * nrows * ncols),
        name="final",
    )(*table, owner, left, right, swapped, top, give, got)


def on_device(nprow, npcol, window, panel, linv, pivots):
    nrows, ncols = window.shape
    nbw = pivots.shape[0]
    nz = nprow // CORES
    columns = [[z * CORES + core for z in range(nz)] for core in range(CORES)]

    def swap(value):
        return lax.ppermute(value, "prow", [(p, p ^ 1) for p in range(nprow)])

    def exchange(value):
        return lax.all_to_all(value, "prow", 0, 0, axis_index_groups=columns, tiled=True)

    def ring(value, size, stride):
        span = size * stride
        pairs = lambda d: [(c, c // span * span + (c + d * stride) % span) for c in range(npcol)]
        return [value] + [lax.ppermute(value, "pcol", pairs(d)) for d in range(1, size)]

    owner = jnp.broadcast_to((pivots // nrows)[:, None], (nbw, LANES))
    count = panel.shape[0]

    own, give, table = pick(pivots, window)
    got = swap(give)
    beside = lax.ppermute(panel, "pcol", [(c, c ^ 1) for c in range(npcol)])
    chip, rows = local(deal_kernel, "deal", ROOMY, [own.shape, (2 * count, nbw)], owner, own, got, panel, beside)
    dealt = exchange(chip)
    kernel = functools.partial(home_kernel, nz)
    line = ring(rows, YS // 2, 2)
    chosen, strip = local(kernel, "home", ROOMY, [own.shape, (YS * count, nbw)], owner, dealt, *line)
    far = exchange(chosen)
    left, right, token = split(linv, ring(strip, npcol // YS, YS))
    (paired,) = local(pair_kernel, "pair", PARAMS, [own.shape], owner, own, far, token)
    last = swap(paired)
    top, swapped = ready(table, owner, own, got, far, window)
    return final(table, owner, left, right, swapped, top, give, last)


def solution(mesh):
    return jax.shard_map(
        functools.partial(on_device, mesh.shape["prow"], mesh.shape["pcol"]),
        mesh=mesh,
        in_specs=(P("prow", "pcol"), P(("prow", "pcol"), None), P(), P()),
        out_specs=P("prow", "pcol"),
        check_vma=False,
    )
```

```python
import functools

import jax
import jax.numpy as jnp
from jax import lax
from jax.experimental import pallas as pl
from jax.experimental.pallas import tpu as pltpu
from jax.sharding import PartitionSpec as P

CORES = 2
LANES = 128
STEP = 256
PARAMS = pltpu.CompilerParams(vmem_limit_bytes=32 * 1024 * 1024)
ROOMY = pltpu.CompilerParams(vmem_limit_bytes=58 * 1024 * 1024)


def vmem(count):
    return [pl.BlockSpec(memory_space=pltpu.VMEM)] * count


def smem(count):
    return [pl.BlockSpec(memory_space=pltpu.SMEM)] * count


def cost(flops, nbytes):
    return pl.CostEstimate(flops=flops, bytes_accessed=nbytes, transcendentals=0)


def tiles(ncols):
    return [slice(c, c + LANES) for c in range(0, ncols, LANES)]


def sides(half):
    me = lax.axis_index("prow")
    core = lax.rem(me, CORES)
    return me, me + 1 - 2 * core, core * half, half - core * half


def each(count, body):
    def four(j, carry):
        for u in range(4):
            body(jnp.minimum(4 * j + u, count - 1))
        return carry

    lax.fori_loop(0, (count + 3) // 4, four, 0)


def pick_kernel(piv, win, panel, own, give, spread, slots, rows, counts, held, sem):
    nrows = win.shape[0]
    half = own.shape[0]
    me, _, base, other = sides(half)
    first = me * nrows
    load = pltpu.make_async_copy(win, held, sem)
    load.start()
    count = panel.shape[0]
    spread[...] = jnp.zeros_like(spread)
    spread[pl.ds(pl.multiple_of(lax.axis_index("pcol") * count, count), count), :] = panel[...]

    def step(i, totals):
        new = []
        for side, start in enumerate((base, other)):
            local = piv[start + i] - first
            inside = (local >= 0) & (local < nrows)
            slots[side, totals[side]] = i
            rows[side, totals[side]] = local
            new.append(totals[side] + inside.astype(jnp.int32))
        return tuple(new)

    totals = lax.fori_loop(0, half, step, (jnp.int32(0), jnp.int32(0)), unroll=8)
    load.wait()
    for side, start, out in ((1, other, give), (0, base, own)):
        counts[side] = totals[side]
        out[...] = held[pl.ds(pl.multiple_of(start, half), half), :]

        def put(i, side=side, out=out):
            out[pl.ds(slots[side, i], 1), :] = held[pl.ds(rows[side, i], 1), :]

        each(totals[side], put)


def pick(pivots, window, panel):
    half = pivots.shape[0] // CORES
    ncols = window.shape[1]
    block = jax.ShapeDtypeStruct((half, ncols), window.dtype)
    table = jax.ShapeDtypeStruct((CORES, half), jnp.int32)
    spread = jax.ShapeDtypeStruct((window.shape[0], panel.shape[1]), panel.dtype)
    out = pl.pallas_call(
        pick_kernel,
        out_shape=(block, block, spread, table, table, jax.ShapeDtypeStruct((CORES,), jnp.int32)),
        in_specs=smem(1) + [pl.BlockSpec(memory_space=pl.ANY)] + vmem(1),
        out_specs=tuple(vmem(3) + smem(3)),
        scratch_shapes=[pltpu.VMEM(window.shape, window.dtype), pltpu.SemaphoreType.DMA],
        compiler_params=ROOMY,
        cost_estimate=cost(0, 16 * half * ncols),
        name="pick",
    )(pivots, window, panel)
    return out[0], out[1], out[2], out[3:]


def half_of(owner, base, half):
    return owner[pl.ds(pl.multiple_of(base, half), half), :]


def deal_kernel(owner, own, got, out):
    half, ncols = own.shape
    me, partner, base, _ = sides(half)
    who = half_of(owner, base, half)
    theirs = (who == partner) | ((who != me) & (who != jnp.where(me == 0, who, -1)))
    for cols in tiles(ncols):
        out[:, cols] = jnp.where(theirs, got[:, cols], own[:, cols])


def home_kernel(nz, owner, got, out):
    half, ncols = got.shape
    part = half // nz
    me, _, base, _ = sides(half)
    at = pl.multiple_of(base + me // CORES * part, part)
    chip = owner[pl.ds(at, part), :] // CORES
    for cols in tiles(ncols):
        former = got[0:part, cols]
        top = former
        for z in range(1, nz):
            top = jnp.where(chip == z, got[z * part : (z + 1) * part, cols], top)
        for z in range(nz):
            out[z * part : (z + 1) * part, cols] = jnp.where(chip == z, former, top)


def pair_kernel(owner, own, got, out):
    half, ncols = own.shape
    me, partner, base, _ = sides(half)
    who = half_of(owner, base, half)
    mine = (who == me) | (who == jnp.where(me == 0, partner, me))
    for cols in tiles(ncols):
        out[:, cols] = jnp.where(mine, own[:, cols], got[:, cols])


def local(kernel, name, params, shapes, *blocks):
    outs = tuple(jax.ShapeDtypeStruct(shape, jnp.float32) for shape in shapes)
    return pl.pallas_call(
        kernel,
        out_shape=outs,
        in_specs=vmem(len(blocks)),
        out_specs=tuple(vmem(len(outs))),
        compiler_params=params,
        cost_estimate=cost(0, 4 * sum(block.size for block in blocks)),
        name=name,
    )(*blocks)


def parts(value):
    high = value.astype(jnp.bfloat16)
    return high, (value - high.astype(jnp.float32)).astype(jnp.bfloat16)


def split_kernel(linv, panel, left, right):
    for source, out in ((linv, left), (panel, right)):
        nb = source.shape[1]
        high, low = parts(source[...])
        out[:, 0:nb] = high
        out[:, nb : 2 * nb] = low
        out[:, 2 * nb : 3 * nb] = high


def split(linv, panel):
    shapes = [jax.ShapeDtypeStruct((a.shape[0], 3 * a.shape[1]), jnp.bfloat16) for a in (linv, panel)]
    return pl.pallas_call(
        split_kernel,
        out_shape=tuple(shapes),
        in_specs=vmem(2),
        out_specs=tuple(vmem(2)),
        compiler_params=PARAMS,
        cost_estimate=cost(0, 10 * (linv.size + panel.size)),
        name="split",
    )(linv, panel)


def ready_kernel(slots, rows, counts, owner, own, got, far, win, top, swapped):
    half, ncols = own.shape
    me, partner, base, other = sides(half)
    who = half_of(owner, base, half)
    for cols in tiles(ncols):
        theirs = jnp.where(who == partner, got[:, cols], far[:, cols])
        top[:, cols] = jnp.where(who == me, own[:, cols], theirs)
    swapped[...] = win[...]

    def put(source, side, start):
        def one(i):
            swapped[pl.ds(rows[side, i], 1), :] = source[pl.ds(start + slots[side, i], 1), :]

        each(counts[side], one)

    @pl.when(me == 0)
    def _():
        put(win, 0, base)
        put(win, 1, other)

    @pl.when(me == 1)
    def _():
        put(got, 0, 0)

    @pl.when(me > 1)
    def _():
        put(far, 0, 0)


def ready(table, owner, own, got, far, window):
    return pl.pallas_call(
        ready_kernel,
        out_shape=(
            jax.ShapeDtypeStruct(own.shape, own.dtype),
            jax.ShapeDtypeStruct(window.shape, window.dtype),
        ),
        in_specs=smem(3) + vmem(5),
        out_specs=tuple(vmem(2)),
        compiler_params=PARAMS,
        cost_estimate=cost(0, 8 * window.size + 16 * own.size),
        name="ready",
    )(*table, owner, own, got, far, window)


def final_kernel(slots, rows, counts, owner, left, right, swapped, top, give, got, out, full, rhs):
    half = top.shape[0]
    nb = 2 * half
    nrows, step = out.shape
    me, _, base, other = sides(half)
    base = pl.multiple_of(base, half)
    other = pl.multiple_of(other, half)
    at = pl.multiple_of(pl.program_id(0) * step, step)
    who = half_of(owner, other, half)
    full[pl.ds(base, half), :] = top[:, pl.ds(at, step)]
    for c in range(0, step, LANES):
        cols = pl.ds(pl.multiple_of(at + c, LANES), LANES)
        full[pl.ds(other, half), c : c + LANES] = jnp.where(who == me, give[:, cols], got[:, cols])

    def product(factor, value):
        high, low = parts(value)
        rhs[0:nb, :] = high
        rhs[nb : 2 * nb, :] = high
        rhs[2 * nb : 3 * nb, :] = low
        return jnp.dot(factor[...], rhs[...], preferred_element_type=jnp.float32)

    out[...] = swapped[:, pl.ds(at, step)]

    def put(i):
        out[pl.ds(rows[1, i], 1), :] = got[pl.ds(slots[1, i], 1), pl.ds(at, step)]

    each(jnp.where(me == 0, 0, counts[1]), put)
    solved = product(left, full[...])
    out[...] = out[...] - product(right, solved)

    @pl.when(me == 0)
    def _():
        out[0:nb, :] = solved


def final(table, owner, left, right, swapped, top, give, got):
    nrows, ncols = swapped.shape
    nb = 2 * top.shape[0]
    step = min(STEP, ncols)
    return pl.pallas_call(
        final_kernel,
        grid=(ncols // step,),
        out_shape=jax.ShapeDtypeStruct(swapped.shape, swapped.dtype),
        in_specs=smem(3) + vmem(7),
        out_specs=pl.BlockSpec((nrows, step), lambda c: (0, c)),
        scratch_shapes=[pltpu.VMEM((nb, step), jnp.float32), pltpu.VMEM((3 * nb, step), jnp.bfloat16)],
        compiler_params=PARAMS,
        cost_estimate=cost(6 * (nb + nrows) * nb * ncols, 8 * nrows * ncols),
        name="final",
    )(*table, owner, left, right, swapped, top, give, got)


def on_device(nprow, window, panel, linv, pivots):
    nrows, ncols = window.shape
    nbw = pivots.shape[0]
    nz = nprow // CORES
    columns = [[z * CORES + core for z in range(nz)] for core in range(CORES)]

    def swap(value):
        return lax.ppermute(value, "prow", [(p, p ^ 1) for p in range(nprow)])

    def exchange(value):
        return lax.all_to_all(value, "prow", 0, 0, axis_index_groups=columns, tiled=True)

    owner = jnp.broadcast_to((pivots // nrows)[:, None], (nbw, LANES))

    own, give, spread, table = pick(pivots, window, panel)
    whole = lax.psum(spread, "pcol")
    got = swap(give)
    (chip,) = local(deal_kernel, "deal", PARAMS, [own.shape], owner, own, got)
    dealt = exchange(chip)
    (chosen,) = local(functools.partial(home_kernel, nz), "home", PARAMS, [own.shape], owner, dealt)
    far = exchange(chosen)
    (paired,) = local(pair_kernel, "pair", PARAMS, [own.shape], owner, own, far)
    last = swap(paired)
    left, right = split(linv, whole)
    top, swapped = ready(table, owner, own, got, far, window)
    return final(table, owner, left, right, swapped, top, give, last)


def solution(mesh):
    return jax.shard_map(
        functools.partial(on_device, mesh.shape["prow"]),
        mesh=mesh,
        in_specs=(P("prow", "pcol"), P(("prow", "pcol"), None), P(), P()),
        out_specs=P("prow", "pcol"),
        check_vma=False,
    )
```

```python
import functools

import jax
import jax.numpy as jnp
from jax import lax
from jax.experimental import pallas as pl
from jax.experimental.pallas import tpu as pltpu
from jax.sharding import PartitionSpec as P

CORES = 2
YS = 8
LANES = 128
STEP = 512
PARAMS = pltpu.CompilerParams(vmem_limit_bytes=32 * 1024 * 1024)
ROOMY = pltpu.CompilerParams(vmem_limit_bytes=58 * 1024 * 1024)


def vmem(count):
    return [pl.BlockSpec(memory_space=pltpu.VMEM)] * count


def smem(count):
    return [pl.BlockSpec(memory_space=pltpu.SMEM)] * count


def cost(flops, nbytes):
    return pl.CostEstimate(flops=flops, bytes_accessed=nbytes, transcendentals=0)


def tiles(ncols):
    return [slice(c, c + LANES) for c in range(0, ncols, LANES)]


def sides(half):
    me = lax.axis_index("prow")
    core = lax.rem(me, CORES)
    return me, me + 1 - 2 * core, core * half, half - core * half


def each(count, body):
    def four(j, carry):
        for u in range(4):
            body(jnp.minimum(4 * j + u, count - 1))
        return carry

    lax.fori_loop(0, (count + 3) // 4, four, 0)


def pick_kernel(piv, win, own, give, slots, rows, counts, held, sem):
    nrows = win.shape[0]
    half = own.shape[0]
    me, _, base, other = sides(half)
    first = me * nrows
    load = pltpu.make_async_copy(win, held, sem)
    load.start()

    def step(i, totals):
        new = []
        for side, start in enumerate((base, other)):
            local = piv[start + i] - first
            inside = (local >= 0) & (local < nrows)
            slots[side, totals[side]] = i
            rows[side, totals[side]] = local
            new.append(totals[side] + inside.astype(jnp.int32))
        return tuple(new)

    totals = lax.fori_loop(0, half, step, (jnp.int32(0), jnp.int32(0)), unroll=8)
    load.wait()
    for side, start, out in ((1, other, give), (0, base, own)):
        counts[side] = totals[side]
        out[...] = held[pl.ds(pl.multiple_of(start, half), half), :]

        def put(i, side=side, out=out):
            out[pl.ds(slots[side, i], 1), :] = held[pl.ds(rows[side, i], 1), :]

        each(totals[side], put)


def pick(pivots, window):
    half = pivots.shape[0] // CORES
    ncols = window.shape[1]
    block = jax.ShapeDtypeStruct((half, ncols), window.dtype)
    table = jax.ShapeDtypeStruct((CORES, half), jnp.int32)
    out = pl.pallas_call(
        pick_kernel,
        out_shape=(block, block, table, table, jax.ShapeDtypeStruct((CORES,), jnp.int32)),
        in_specs=smem(1) + [pl.BlockSpec(memory_space=pl.ANY)],
        out_specs=tuple(vmem(2) + smem(3)),
        scratch_shapes=[pltpu.VMEM(window.shape, window.dtype), pltpu.SemaphoreType.DMA],
        compiler_params=ROOMY,
        cost_estimate=cost(0, 16 * half * ncols),
        name="pick",
    )(pivots, window)
    return out[0], out[1], out[2:]


def half_of(owner, base, half):
    return owner[pl.ds(pl.multiple_of(base, half), half), :]


def deal_kernel(owner, own, got, panel, beside, out, rows):
    half, ncols = own.shape
    me, partner, base, _ = sides(half)
    who = half_of(owner, base, half)
    theirs = (who == partner) | ((who != me) & (who != jnp.where(me == 0, who, -1)))
    for cols in tiles(ncols):
        out[:, cols] = jnp.where(theirs, got[:, cols], own[:, cols])
    stack(4, panel, beside, rows)


def bit(weight):
    return lax.rem(lax.axis_index("pcol") // weight, 2)


def stack(weight, mine, theirs, out):
    count = mine.shape[0]
    for block, side in ((mine, bit(weight)), (theirs, 1 - bit(weight))):
        out[pl.ds(pl.multiple_of(side * count, count), count), :] = block[...]


def join_kernel(mine, theirs, out):
    stack(1, mine, theirs, out)


def ordered(index, pieces, put):
    count = pieces[0].shape[0]
    for d, piece in enumerate(pieces):
        source = lax.rem(index - d + len(pieces), len(pieces))
        put(pl.ds(pl.multiple_of(source * count, count), count), piece[...])


def home_kernel(nz, owner, got, mine, theirs, out, strip):
    half, ncols = got.shape
    part = half // nz
    me, _, base, _ = sides(half)
    at = pl.multiple_of(base + me // CORES * part, part)
    chip = owner[pl.ds(at, part), :] // CORES
    for cols in tiles(ncols):
        former = got[0:part, cols]
        top = former
        for z in range(1, nz):
            top = jnp.where(chip == z, got[z * part : (z + 1) * part, cols], top)
        for z in range(nz):
            out[z * part : (z + 1) * part, cols] = jnp.where(chip == z, former, top)

    count = mine.shape[0] // 4
    for block, side in ((mine, bit(2)), (theirs, 1 - bit(2))):
        for i in range(4):
            at = pl.multiple_of((4 * (i % 2) + 2 * side + i // 2) * count, count)
            strip[pl.ds(at, count), :] = block[i * count : (i + 1) * count, :]


def pair_kernel(owner, own, got, *refs):
    out = refs[-1]
    half, ncols = own.shape
    me, partner, base, _ = sides(half)
    who = half_of(owner, base, half)
    mine = (who == me) | (who == jnp.where(me == 0, partner, me))
    for cols in tiles(ncols):
        out[:, cols] = jnp.where(mine, own[:, cols], got[:, cols])


def local(kernel, name, params, shapes, *blocks, after=()):
    outs = tuple(jax.ShapeDtypeStruct(shape, jnp.float32) for shape in shapes)
    return pl.pallas_call(
        kernel,
        out_shape=outs,
        in_specs=vmem(len(blocks)) + [pl.BlockSpec(memory_space=pl.ANY)] * len(after),
        out_specs=tuple(vmem(len(outs))),
        compiler_params=params,
        cost_estimate=cost(0, 4 * sum(block.size for block in blocks)),
        name=name,
    )(*blocks, *after)


def parts(value):
    high = value.astype(jnp.bfloat16)
    return high, (value - high.astype(jnp.float32)).astype(jnp.bfloat16)


def split_kernel(linv, *refs):
    strips, (left, right) = refs[:-2], refs[-2:]
    nb = linv.shape[1]

    def put(value, out, rows):
        high, low = parts(value)
        out[rows, 0:nb] = high
        out[rows, nb : 2 * nb] = low
        out[rows, 2 * nb : 3 * nb] = high

    put(linv[...], left, slice(None))
    ordered(lax.axis_index("pcol") // YS, strips, lambda rows, value: put(value, right, rows))


def split(linv, strips):
    nb = linv.shape[1]
    nrows = sum(strip.shape[0] for strip in strips)
    return pl.pallas_call(
        split_kernel,
        out_shape=(
            jax.ShapeDtypeStruct((nb, 3 * nb), jnp.bfloat16),
            jax.ShapeDtypeStruct((nrows, 3 * nb), jnp.bfloat16),
        ),
        in_specs=vmem(1 + len(strips)),
        out_specs=tuple(vmem(2)),
        compiler_params=PARAMS,
        cost_estimate=cost(0, 10 * nb * (nb + nrows)),
        name="split",
    )(linv, *strips)


def ready_kernel(slots, rows, counts, owner, own, got, far, win, top, swapped):
    half, ncols = own.shape
    me, partner, base, other = sides(half)
    who = half_of(owner, base, half)
    for cols in tiles(ncols):
        theirs = jnp.where(who == partner, got[:, cols], far[:, cols])
        top[:, cols] = jnp.where(who == me, own[:, cols], theirs)
    swapped[...] = win[...]

    def put(source, side, start):
        def one(i):
            swapped[pl.ds(rows[side, i], 1), :] = source[pl.ds(start + slots[side, i], 1), :]

        each(counts[side], one)

    @pl.when(me == 0)
    def _():
        put(win, 0, base)
        put(win, 1, other)

    @pl.when(me == 1)
    def _():
        put(got, 0, 0)

    @pl.when(me > 1)
    def _():
        put(far, 0, 0)


def ready(table, owner, own, got, far, window):
    return pl.pallas_call(
        ready_kernel,
        out_shape=(
            jax.ShapeDtypeStruct(own.shape, own.dtype),
            jax.ShapeDtypeStruct(window.shape, window.dtype),
        ),
        in_specs=smem(3) + vmem(5),
        out_specs=tuple(vmem(2)),
        compiler_params=PARAMS,
        cost_estimate=cost(0, 8 * window.size + 16 * own.size),
        name="ready",
    )(*table, owner, own, got, far, window)


def final_kernel(slots, rows, counts, owner, left, right, swapped, top, give, got, out, full, rhs):
    half = top.shape[0]
    nb = 2 * half
    nrows, step = out.shape
    me, _, base, other = sides(half)
    base = pl.multiple_of(base, half)
    other = pl.multiple_of(other, half)
    at = pl.multiple_of(pl.program_id(0) * step, step)
    who = half_of(owner, other, half)
    full[pl.ds(base, half), :] = top[:, pl.ds(at, step)]
    for c in range(0, step, LANES):
        cols = pl.ds(pl.multiple_of(at + c, LANES), LANES)
        full[pl.ds(other, half), c : c + LANES] = jnp.where(who == me, give[:, cols], got[:, cols])

    def product(factor, value):
        high, low = parts(value)
        rhs[0:nb, :] = high
        rhs[nb : 2 * nb, :] = high
        rhs[2 * nb : 3 * nb, :] = low
        return jnp.dot(factor[...], rhs[...], preferred_element_type=jnp.float32)

    out[...] = swapped[:, pl.ds(at, step)]

    def put(i):
        out[pl.ds(rows[1, i], 1), :] = got[pl.ds(slots[1, i], 1), pl.ds(at, step)]

    each(jnp.where(me == 0, 0, counts[1]), put)
    solved = product(left, full[...])
    out[...] = out[...] - product(right, solved)

    @pl.when(me == 0)
    def _():
        out[0:nb, :] = solved


def final(table, owner, left, right, swapped, top, give, got):
    nrows, ncols = swapped.shape
    nb = 2 * top.shape[0]
    step = min(STEP, ncols)
    return pl.pallas_call(
        final_kernel,
        grid=(ncols // step,),
        out_shape=jax.ShapeDtypeStruct(swapped.shape, swapped.dtype),
        in_specs=smem(3) + vmem(7),
        out_specs=pl.BlockSpec((nrows, step), lambda c: (0, c)),
        scratch_shapes=[pltpu.VMEM((nb, step), jnp.float32), pltpu.VMEM((3 * nb, step), jnp.bfloat16)],
        compiler_params=PARAMS,
        cost_estimate=cost(6 * (nb + nrows) * nb * ncols, 8 * nrows * ncols),
        name="final",
    )(*table, owner, left, right, swapped, top, give, got)


def on_device(nprow, npcol, window, panel, linv, pivots):
    nrows, ncols = window.shape
    nbw = pivots.shape[0]
    nz = nprow // CORES
    columns = [[z * CORES + core for z in range(nz)] for core in range(CORES)]

    def swap(value):
        return lax.ppermute(value, "prow", [(p, p ^ 1) for p in range(nprow)])

    def exchange(value):
        return lax.all_to_all(value, "prow", 0, 0, axis_index_groups=columns, tiled=True)

    def across(value, weight):
        return lax.ppermute(value, "pcol", [(c, c ^ weight) for c in range(npcol)])

    def ring(value, size, stride):
        span = size * stride
        pairs = lambda d: [(c, c // span * span + (c + d * stride) % span) for c in range(npcol)]
        return [value] + [lax.ppermute(value, "pcol", pairs(d)) for d in range(1, size)]

    owner = jnp.broadcast_to((pivots // nrows)[:, None], (nbw, LANES))
    count = panel.shape[0]

    own, give, table = pick(pivots, window)
    got = swap(give)
    beside = across(panel, 4)
    chip, rows = local(deal_kernel, "deal", PARAMS, [own.shape, (2 * count, nbw)], owner, own, got, panel, beside)
    dealt = exchange(chip)
    (mine,) = local(join_kernel, "join", PARAMS, [(4 * count, nbw)], rows, across(rows, 1))
    kernel, shapes = functools.partial(home_kernel, nz), [own.shape, (YS * count, nbw)]
    chosen, strip = local(kernel, "home", ROOMY, shapes, owner, dealt, mine, across(mine, 2))
    far = exchange(chosen)
    strips = ring(strip, npcol // YS, YS)
    (paired,) = local(pair_kernel, "pair", PARAMS, [own.shape], owner, own, far, after=strips[1:])
    last = swap(paired)
    left, right = split(linv, strips)
    top, swapped = ready(table, owner, own, got, far, window)
    return final(table, owner, left, right, swapped, top, give, last)


def solution(mesh):
    return jax.shard_map(
        functools.partial(on_device, mesh.shape["prow"], mesh.shape["pcol"]),
        mesh=mesh,
        in_specs=(P("prow", "pcol"), P(("prow", "pcol"), None), P(), P()),
        out_specs=P("prow", "pcol"),
        check_vma=False,
    )
```

```python
import functools

import jax
import jax.numpy as jnp
from jax import lax
from jax.experimental import pallas as pl
from jax.experimental.pallas import tpu as pltpu
from jax.sharding import PartitionSpec as P

CORES = 2
YS = 8
LANES = 128
STEP = 512
PARAMS = pltpu.CompilerParams(vmem_limit_bytes=32 * 1024 * 1024)
ROOMY = pltpu.CompilerParams(vmem_limit_bytes=58 * 1024 * 1024)


def vmem(count):
    return [pl.BlockSpec(memory_space=pltpu.VMEM)] * count


def smem(count):
    return [pl.BlockSpec(memory_space=pltpu.SMEM)] * count


def cost(flops, nbytes):
    return pl.CostEstimate(flops=flops, bytes_accessed=nbytes, transcendentals=0)


def tiles(ncols):
    return [slice(c, c + LANES) for c in range(0, ncols, LANES)]


def sides(half):
    me = lax.axis_index("prow")
    core = lax.rem(me, CORES)
    return me, me + 1 - 2 * core, core * half, half - core * half


def each(count, body):
    def four(j, carry):
        for u in range(4):
            body(jnp.minimum(4 * j + u, count - 1))
        return carry

    lax.fori_loop(0, (count + 3) // 4, four, 0)


def pick_kernel(piv, win, own, give, slots, rows, counts, held, sem):
    nrows = win.shape[0]
    half = own.shape[0]
    me, _, base, other = sides(half)
    first = me * nrows
    load = pltpu.make_async_copy(win, held, sem)
    load.start()

    def step(i, totals):
        new = []
        for side, start in enumerate((base, other)):
            local = piv[start + i] - first
            inside = (local >= 0) & (local < nrows)
            slots[side, totals[side]] = i
            rows[side, totals[side]] = local
            new.append(totals[side] + inside.astype(jnp.int32))
        return tuple(new)

    totals = lax.fori_loop(0, half, step, (jnp.int32(0), jnp.int32(0)), unroll=8)
    load.wait()
    for side, start, out in ((1, other, give), (0, base, own)):
        counts[side] = totals[side]
        out[...] = held[pl.ds(pl.multiple_of(start, half), half), :]

        def put(i, side=side, out=out):
            out[pl.ds(slots[side, i], 1), :] = held[pl.ds(rows[side, i], 1), :]

        each(totals[side], put)


def pick(pivots, window):
    half = pivots.shape[0] // CORES
    ncols = window.shape[1]
    block = jax.ShapeDtypeStruct((half, ncols), window.dtype)
    table = jax.ShapeDtypeStruct((CORES, half), jnp.int32)
    out = pl.pallas_call(
        pick_kernel,
        out_shape=(block, block, table, table, jax.ShapeDtypeStruct((CORES,), jnp.int32)),
        in_specs=smem(1) + [pl.BlockSpec(memory_space=pl.ANY)],
        out_specs=tuple(vmem(2) + smem(3)),
        scratch_shapes=[pltpu.VMEM(window.shape, window.dtype), pltpu.SemaphoreType.DMA],
        compiler_params=ROOMY,
        cost_estimate=cost(0, 16 * half * ncols),
        name="pick",
    )(pivots, window)
    return out[0], out[1], out[2:]


def half_of(owner, base, half):
    return owner[pl.ds(pl.multiple_of(base, half), half), :]


def deal_kernel(owner, own, got, panel, beside, out, rows):
    half, ncols = own.shape
    me, partner, base, _ = sides(half)
    who = half_of(owner, base, half)
    theirs = (who == partner) | ((who != me) & (who != jnp.where(me == 0, who, -1)))
    for cols in tiles(ncols):
        out[:, cols] = jnp.where(theirs, got[:, cols], own[:, cols])
    stack(4, panel, beside, rows)


def bit(weight):
    return lax.rem(lax.axis_index("pcol") // weight, 2)


def stack(weight, mine, theirs, out):
    count = mine.shape[0]
    for block, side in ((mine, bit(weight)), (theirs, 1 - bit(weight))):
        out[pl.ds(pl.multiple_of(side * count, count), count), :] = block[...]


def join_kernel(mine, theirs, out):
    stack(1, mine, theirs, out)


def ordered(index, pieces, put):
    count = pieces[0].shape[0]
    for d, piece in enumerate(pieces):
        source = lax.rem(index - d + len(pieces), len(pieces))
        put(pl.ds(pl.multiple_of(source * count, count), count), piece[...])


def home_kernel(nz, nrows, piv, got, mine, theirs, out, strip):
    half, ncols = got.shape
    part = half // nz
    me, _, base, _ = sides(half)
    at = base + me // CORES * part
    slot = lax.broadcasted_iota(jnp.int32, (part, LANES), 0)
    chip = jnp.zeros((part, LANES), jnp.int32)
    for i in range(part):
        chip = jnp.where(slot == i, piv[at + i] // (nrows * CORES), chip)
    for cols in tiles(ncols):
        former = got[0:part, cols]
        top = former
        for z in range(1, nz):
            top = jnp.where(chip == z, got[z * part : (z + 1) * part, cols], top)
        for z in range(nz):
            out[z * part : (z + 1) * part, cols] = jnp.where(chip == z, former, top)

    count = mine.shape[0] // 4
    for block, side in ((mine, bit(2)), (theirs, 1 - bit(2))):
        for i in range(4):
            at = pl.multiple_of((4 * (i % 2) + 2 * side + i // 2) * count, count)
            strip[pl.ds(at, count), :] = block[i * count : (i + 1) * count, :]


def pair_kernel(owner, own, got, *refs):
    out = refs[-1]
    half, ncols = own.shape
    me, partner, base, _ = sides(half)
    who = half_of(owner, base, half)
    mine = (who == me) | (who == jnp.where(me == 0, partner, me))
    for cols in tiles(ncols):
        out[:, cols] = jnp.where(mine, own[:, cols], got[:, cols])


def local(kernel, name, params, shapes, *blocks, scalars=(), after=()):
    outs = tuple(jax.ShapeDtypeStruct(shape, jnp.float32) for shape in shapes)
    return pl.pallas_call(
        kernel,
        out_shape=outs,
        in_specs=smem(len(scalars)) + vmem(len(blocks)) + [pl.BlockSpec(memory_space=pl.ANY)] * len(after),
        out_specs=tuple(vmem(len(outs))),
        compiler_params=params,
        cost_estimate=cost(0, 4 * sum(block.size for block in blocks)),
        name=name,
    )(*scalars, *blocks, *after)


def parts(value):
    high = value.astype(jnp.bfloat16)
    return high, (value - high.astype(jnp.float32)).astype(jnp.bfloat16)


def split_kernel(linv, *refs):
    strips, (left, right) = refs[:-2], refs[-2:]
    nb = linv.shape[1]

    def put(value, out, rows):
        high, low = parts(value)
        out[rows, 0:nb] = high
        out[rows, nb : 2 * nb] = low
        out[rows, 2 * nb : 3 * nb] = high

    put(linv[...], left, slice(None))
    ordered(lax.axis_index("pcol") // YS, strips, lambda rows, value: put(value, right, rows))


def split(linv, strips):
    nb = linv.shape[1]
    nrows = sum(strip.shape[0] for strip in strips)
    return pl.pallas_call(
        split_kernel,
        out_shape=(
            jax.ShapeDtypeStruct((nb, 3 * nb), jnp.bfloat16),
            jax.ShapeDtypeStruct((nrows, 3 * nb), jnp.bfloat16),
        ),
        in_specs=vmem(1 + len(strips)),
        out_specs=tuple(vmem(2)),
        compiler_params=PARAMS,
        cost_estimate=cost(0, 10 * nb * (nb + nrows)),
        name="split",
    )(linv, *strips)


def ready_kernel(slots, rows, counts, owner, own, got, far, win, top, swapped):
    half, ncols = own.shape
    me, partner, base, other = sides(half)
    who = half_of(owner, base, half)
    for cols in tiles(ncols):
        theirs = jnp.where(who == partner, got[:, cols], far[:, cols])
        top[:, cols] = jnp.where(who == me, own[:, cols], theirs)
    swapped[...] = win[...]

    def put(source, side, start):
        def one(i):
            swapped[pl.ds(rows[side, i], 1), :] = source[pl.ds(start + slots[side, i], 1), :]

        each(counts[side], one)

    @pl.when(me == 0)
    def _():
        put(win, 0, base)
        put(win, 1, other)

    @pl.when(me == 1)
    def _():
        put(got, 0, 0)

    @pl.when(me > 1)
    def _():
        put(far, 0, 0)


def ready(table, owner, own, got, far, window):
    return pl.pallas_call(
        ready_kernel,
        out_shape=(
            jax.ShapeDtypeStruct(own.shape, own.dtype),
            jax.ShapeDtypeStruct(window.shape, window.dtype),
        ),
        in_specs=smem(3) + vmem(5),
        out_specs=tuple(vmem(2)),
        compiler_params=PARAMS,
        cost_estimate=cost(0, 8 * window.size + 16 * own.size),
        name="ready",
    )(*table, owner, own, got, far, window)


def final_kernel(slots, rows, counts, owner, left, right, swapped, top, give, got, out, full, rhs):
    half = top.shape[0]
    nb = 2 * half
    nrows, step = out.shape
    me, _, base, other = sides(half)
    base = pl.multiple_of(base, half)
    other = pl.multiple_of(other, half)
    at = pl.multiple_of(pl.program_id(0) * step, step)
    who = half_of(owner, other, half)
    full[pl.ds(base, half), :] = top[:, pl.ds(at, step)]
    for c in range(0, step, LANES):
        cols = pl.ds(pl.multiple_of(at + c, LANES), LANES)
        full[pl.ds(other, half), c : c + LANES] = jnp.where(who == me, give[:, cols], got[:, cols])

    def product(factor, value):
        high, low = parts(value)
        rhs[0:nb, :] = high
        rhs[nb : 2 * nb, :] = high
        rhs[2 * nb : 3 * nb, :] = low
        return jnp.dot(factor[...], rhs[...], preferred_element_type=jnp.float32)

    out[...] = swapped[:, pl.ds(at, step)]

    def put(i):
        out[pl.ds(rows[1, i], 1), :] = got[pl.ds(slots[1, i], 1), pl.ds(at, step)]

    each(jnp.where(me == 0, 0, counts[1]), put)
    solved = product(left, full[...])
    out[...] = out[...] - product(right, solved)

    @pl.when(me == 0)
    def _():
        out[0:nb, :] = solved


def final(table, owner, left, right, swapped, top, give, got):
    nrows, ncols = swapped.shape
    nb = 2 * top.shape[0]
    step = min(STEP, ncols)
    return pl.pallas_call(
        final_kernel,
        grid=(ncols // step,),
        out_shape=jax.ShapeDtypeStruct(swapped.shape, swapped.dtype),
        in_specs=smem(3) + vmem(7),
        out_specs=pl.BlockSpec((nrows, step), lambda c: (0, c)),
        scratch_shapes=[pltpu.VMEM((nb, step), jnp.float32), pltpu.VMEM((3 * nb, step), jnp.bfloat16)],
        compiler_params=PARAMS,
        cost_estimate=cost(6 * (nb + nrows) * nb * ncols, 8 * nrows * ncols),
        name="final",
    )(*table, owner, left, right, swapped, top, give, got)


def on_device(nprow, npcol, window, panel, linv, pivots):
    nrows, ncols = window.shape
    nbw = pivots.shape[0]
    nz = nprow // CORES
    columns = [[z * CORES + core for z in range(nz)] for core in range(CORES)]

    def swap(value):
        return lax.ppermute(value, "prow", [(p, p ^ 1) for p in range(nprow)])

    def exchange(value):
        return lax.all_to_all(value, "prow", 0, 0, axis_index_groups=columns, tiled=True)

    def across(value, weight):
        return lax.ppermute(value, "pcol", [(c, c ^ weight) for c in range(npcol)])

    def ring(value, size, stride):
        span = size * stride
        pairs = lambda d: [(c, c // span * span + (c + d * stride) % span) for c in range(npcol)]
        return [value] + [lax.ppermute(value, "pcol", pairs(d)) for d in range(1, size)]

    owner = jnp.broadcast_to((pivots // nrows)[:, None], (nbw, LANES))
    count = panel.shape[0]

    own, give, table = pick(pivots, window)
    give, beside = lax.optimization_barrier((give, across(panel, 4)))
    got = swap(give)
    chip, rows = local(deal_kernel, "deal", PARAMS, [own.shape, (2 * count, nbw)], owner, own, got, panel, beside)
    dealt = exchange(chip)
    (mine,) = local(join_kernel, "join", PARAMS, [(4 * count, nbw)], rows, across(rows, 1))
    kernel, shapes = functools.partial(home_kernel, nz, nrows), [own.shape, (YS * count, nbw)]
    chosen, strip = local(
        kernel, "home", ROOMY, shapes, dealt, mine, across(mine, 2), scalars=(pivots,)
    )
    far = exchange(chosen)
    strips = ring(strip, npcol // YS, YS)
    (paired,) = local(pair_kernel, "pair", PARAMS, [own.shape], owner, own, far, after=strips[1:])
    last = swap(paired)
    left, right = split(linv, strips)
    top, swapped = ready(table, owner, own, got, far, window)
    return final(table, owner, left, right, swapped, top, give, last)


def solution(mesh):
    return jax.shard_map(
        functools.partial(on_device, mesh.shape["prow"], mesh.shape["pcol"]),
        mesh=mesh,
        in_specs=(P("prow", "pcol"), P(("prow", "pcol"), None), P(), P()),
        out_specs=P("prow", "pcol"),
        check_vma=False,
    )
```

```python
import functools

import jax
import jax.numpy as jnp
from jax import lax
from jax.experimental import pallas as pl
from jax.experimental.pallas import tpu as pltpu
from jax.sharding import PartitionSpec as P

CORES = 2
YS = 8
LANES = 128
STEP = 512
PARAMS = pltpu.CompilerParams(vmem_limit_bytes=32 * 1024 * 1024)
ROOMY = pltpu.CompilerParams(vmem_limit_bytes=58 * 1024 * 1024)


def vmem(count):
    return [pl.BlockSpec(memory_space=pltpu.VMEM)] * count


def smem(count):
    return [pl.BlockSpec(memory_space=pltpu.SMEM)] * count


def cost(flops, nbytes):
    return pl.CostEstimate(flops=flops, bytes_accessed=nbytes, transcendentals=0)


def tiles(ncols):
    return [slice(c, c + LANES) for c in range(0, ncols, LANES)]


def sides(half):
    me = lax.axis_index("prow")
    core = lax.rem(me, CORES)
    return me, me + 1 - 2 * core, core * half, half - core * half


def each(count, body):
    def four(j, carry):
        for u in range(4):
            body(jnp.minimum(4 * j + u, count - 1))
        return carry

    lax.fori_loop(0, (count + 3) // 4, four, 0)


def pick_kernel(piv, win, own, give, slots, rows, counts, held, sem):
    nrows = win.shape[0]
    half = own.shape[0]
    me, _, base, other = sides(half)
    first = me * nrows
    load = pltpu.make_async_copy(win, held, sem)
    load.start()

    def step(i, totals):
        new = []
        for side, start in enumerate((base, other)):
            local = piv[start + i] - first
            inside = (local >= 0) & (local < nrows)
            slots[side, totals[side]] = i
            rows[side, totals[side]] = local
            new.append(totals[side] + inside.astype(jnp.int32))
        return tuple(new)

    totals = lax.fori_loop(0, half, step, (jnp.int32(0), jnp.int32(0)), unroll=8)
    load.wait()
    for side, start, out in ((1, other, give), (0, base, own)):
        counts[side] = totals[side]
        out[...] = held[pl.ds(pl.multiple_of(start, half), half), :]

        def put(i, side=side, out=out):
            out[pl.ds(slots[side, i], 1), :] = held[pl.ds(rows[side, i], 1), :]

        each(totals[side], put)


def pick(pivots, window):
    half = pivots.shape[0] // CORES
    ncols = window.shape[1]
    block = jax.ShapeDtypeStruct((half, ncols), window.dtype)
    table = jax.ShapeDtypeStruct((CORES, half), jnp.int32)
    out = pl.pallas_call(
        pick_kernel,
        out_shape=(block, block, table, table, jax.ShapeDtypeStruct((CORES,), jnp.int32)),
        in_specs=smem(1) + [pl.BlockSpec(memory_space=pl.ANY)],
        out_specs=tuple(vmem(2) + smem(3)),
        scratch_shapes=[pltpu.VMEM(window.shape, window.dtype), pltpu.SemaphoreType.DMA],
        compiler_params=ROOMY,
        cost_estimate=cost(0, 16 * half * ncols),
        name="pick",
    )(pivots, window)
    return out[0], out[1], out[2:]


def half_of(owner, base, half):
    return owner[pl.ds(pl.multiple_of(base, half), half), :]


def deal_kernel(owner, own, got, out):
    half, ncols = own.shape
    me, partner, base, _ = sides(half)
    who = half_of(owner, base, half)
    theirs = (who == partner) | ((who != me) & (who != jnp.where(me == 0, who, -1)))
    for cols in tiles(ncols):
        out[:, cols] = jnp.where(theirs, got[:, cols], own[:, cols])


def bit(weight):
    return lax.rem(lax.axis_index("pcol") // weight, 2)


def stack(weight, mine, theirs, out):
    count = mine.shape[0]
    for block, side in ((mine, bit(weight)), (theirs, 1 - bit(weight))):
        out[pl.ds(pl.multiple_of(side * count, count), count), :] = block[...]


def join_kernel(weight, mine, theirs, *refs):
    stack(weight, mine, theirs, refs[-1])


def ordered(index, pieces, put):
    count = pieces[0].shape[0]
    for d, piece in enumerate(pieces):
        source = lax.rem(index - d + len(pieces), len(pieces))
        put(pl.ds(pl.multiple_of(source * count, count), count), piece[...])


def home_kernel(nz, nrows, piv, got, mine, theirs, out, strip):
    half, ncols = got.shape
    part = half // nz
    me, _, base, _ = sides(half)
    at = base + me // CORES * part
    slot = lax.broadcasted_iota(jnp.int32, (part, LANES), 0)
    chip = jnp.zeros((part, LANES), jnp.int32)
    for i in range(part):
        chip = jnp.where(slot == i, piv[at + i] // (nrows * CORES), chip)
    for cols in tiles(ncols):
        former = got[0:part, cols]
        top = former
        for z in range(1, nz):
            top = jnp.where(chip == z, got[z * part : (z + 1) * part, cols], top)
        for z in range(nz):
            out[z * part : (z + 1) * part, cols] = jnp.where(chip == z, former, top)

    count = mine.shape[0] // 4
    for block, side in ((mine, bit(2)), (theirs, 1 - bit(2))):
        for i in range(4):
            at = pl.multiple_of((4 * (i % 2) + 2 * side + i // 2) * count, count)
            strip[pl.ds(at, count), :] = block[i * count : (i + 1) * count, :]


def mark_kernel(*refs):
    refs[-1][...] = jnp.zeros_like(refs[-1])


def pair_kernel(owner, own, got, *refs):
    out = refs[-1]
    half, ncols = own.shape
    me, partner, base, _ = sides(half)
    who = half_of(owner, base, half)
    mine = (who == me) | (who == jnp.where(me == 0, partner, me))
    for cols in tiles(ncols):
        out[:, cols] = jnp.where(mine, own[:, cols], got[:, cols])


def local(kernel, name, params, shapes, *blocks, scalars=(), after=()):
    outs = tuple(jax.ShapeDtypeStruct(shape, jnp.float32) for shape in shapes)
    return pl.pallas_call(
        kernel,
        out_shape=outs,
        in_specs=smem(len(scalars)) + vmem(len(blocks)) + [pl.BlockSpec(memory_space=pl.ANY)] * len(after),
        out_specs=tuple(vmem(len(outs))),
        compiler_params=params,
        cost_estimate=cost(0, 4 * sum(block.size for block in blocks)),
        name=name,
    )(*scalars, *blocks, *after)


def parts(value):
    high = value.astype(jnp.bfloat16)
    return high, (value - high.astype(jnp.float32)).astype(jnp.bfloat16)


def split_kernel(linv, *refs):
    strips, (left, right) = refs[:-2], refs[-2:]
    nb = linv.shape[1]

    def put(value, out, rows):
        high, low = parts(value)
        out[rows, 0:nb] = high
        out[rows, nb : 2 * nb] = low
        out[rows, 2 * nb : 3 * nb] = high

    put(linv[...], left, slice(None))
    ordered(lax.axis_index("pcol") // YS, strips, lambda rows, value: put(value, right, rows))


def split(linv, strips):
    nb = linv.shape[1]
    nrows = sum(strip.shape[0] for strip in strips)
    return pl.pallas_call(
        split_kernel,
        out_shape=(
            jax.ShapeDtypeStruct((nb, 3 * nb), jnp.bfloat16),
            jax.ShapeDtypeStruct((nrows, 3 * nb), jnp.bfloat16),
        ),
        in_specs=vmem(1 + len(strips)),
        out_specs=tuple(vmem(2)),
        compiler_params=PARAMS,
        cost_estimate=cost(0, 10 * nb * (nb + nrows)),
        name="split",
    )(linv, *strips)


def ready_kernel(slots, rows, counts, owner, own, got, far, win, top, swapped):
    half, ncols = own.shape
    me, partner, base, other = sides(half)
    who = half_of(owner, base, half)
    for cols in tiles(ncols):
        theirs = jnp.where(who == partner, got[:, cols], far[:, cols])
        top[:, cols] = jnp.where(who == me, own[:, cols], theirs)
    swapped[...] = win[...]

    def put(source, side, start):
        def one(i):
            swapped[pl.ds(rows[side, i], 1), :] = source[pl.ds(start + slots[side, i], 1), :]

        each(counts[side], one)

    @pl.when(me == 0)
    def _():
        put(win, 0, base)
        put(win, 1, other)

    @pl.when(me == 1)
    def _():
        put(got, 0, 0)

    @pl.when(me > 1)
    def _():
        put(far, 0, 0)


def ready(table, owner, own, got, far, window):
    return pl.pallas_call(
        ready_kernel,
        out_shape=(
            jax.ShapeDtypeStruct(own.shape, own.dtype),
            jax.ShapeDtypeStruct(window.shape, window.dtype),
        ),
        in_specs=smem(3) + vmem(5),
        out_specs=tuple(vmem(2)),
        compiler_params=PARAMS,
        cost_estimate=cost(0, 8 * window.size + 16 * own.size),
        name="ready",
    )(*table, owner, own, got, far, window)


def final_kernel(slots, rows, counts, owner, left, right, swapped, top, give, got, out, full, rhs):
    half = top.shape[0]
    nb = 2 * half
    nrows, step = out.shape
    me, _, base, other = sides(half)
    base = pl.multiple_of(base, half)
    other = pl.multiple_of(other, half)
    at = pl.multiple_of(pl.program_id(0) * step, step)
    who = half_of(owner, other, half)
    full[pl.ds(base, half), :] = top[:, pl.ds(at, step)]
    for c in range(0, step, LANES):
        cols = pl.ds(pl.multiple_of(at + c, LANES), LANES)
        full[pl.ds(other, half), c : c + LANES] = jnp.where(who == me, give[:, cols], got[:, cols])

    def product(factor, value):
        high, low = parts(value)
        rhs[0:nb, :] = high
        rhs[nb : 2 * nb, :] = high
        rhs[2 * nb : 3 * nb, :] = low
        return jnp.dot(factor[...], rhs[...], preferred_element_type=jnp.float32)

    out[...] = swapped[:, pl.ds(at, step)]

    def put(i):
        out[pl.ds(rows[1, i], 1), :] = got[pl.ds(slots[1, i], 1), pl.ds(at, step)]

    each(jnp.where(me == 0, 0, counts[1]), put)
    solved = product(left, full[...])
    out[...] = out[...] - product(right, solved)

    @pl.when(me == 0)
    def _():
        out[0:nb, :] = solved


def final(table, owner, left, right, swapped, top, give, got):
    nrows, ncols = swapped.shape
    nb = 2 * top.shape[0]
    step = min(STEP, ncols)
    return pl.pallas_call(
        final_kernel,
        grid=(ncols // step,),
        out_shape=jax.ShapeDtypeStruct(swapped.shape, swapped.dtype),
        in_specs=smem(3) + vmem(7),
        out_specs=pl.BlockSpec((nrows, step), lambda c: (0, c)),
        scratch_shapes=[pltpu.VMEM((nb, step), jnp.float32), pltpu.VMEM((3 * nb, step), jnp.bfloat16)],
        compiler_params=PARAMS,
        cost_estimate=cost(6 * (nb + nrows) * nb * ncols, 8 * nrows * ncols),
        name="final",
    )(*table, owner, left, right, swapped, top, give, got)


def on_device(nprow, npcol, window, panel, linv, pivots):
    nrows, ncols = window.shape
    nbw = pivots.shape[0]
    nz = nprow // CORES
    columns = [[z * CORES + core for z in range(nz)] for core in range(CORES)]

    def swap(value):
        return lax.ppermute(value, "prow", [(p, p ^ 1) for p in range(nprow)])

    def exchange(value):
        return lax.all_to_all(value, "prow", 0, 0, axis_index_groups=columns, tiled=True)

    def across(value, weight):
        return lax.ppermute(value, "pcol", [(c, c ^ weight) for c in range(npcol)])

    def ring(value, size, stride):
        span = size * stride
        pairs = lambda d: [(c, c // span * span + (c + d * stride) % span) for c in range(npcol)]
        return [value] + [lax.ppermute(value, "pcol", pairs(d)) for d in range(1, size)]

    owner = jnp.broadcast_to((pivots // nrows)[:, None], (nbw, LANES))
    count = panel.shape[0]

    own, give, table = pick(pivots, window)
    got = swap(give)
    beside = across(panel, 4)
    (chip,) = local(deal_kernel, "deal", PARAMS, [own.shape], owner, own, got)
    dealt = exchange(chip)
    first, second = functools.partial(join_kernel, 4), functools.partial(join_kernel, 1)
    (rows,) = local(first, "join", PARAMS, [(2 * count, nbw)], panel, beside, after=(chip,))
    (mine,) = local(second, "join", PARAMS, [(4 * count, nbw)], rows, across(rows, 1))
    kernel, shapes = functools.partial(home_kernel, nz, nrows), [own.shape, (YS * count, nbw)]
    chosen, strip = local(
        kernel, "home", ROOMY, shapes, dealt, mine, across(mine, 2), scalars=(pivots,)
    )
    far = exchange(chosen)
    strips = ring(strip, npcol // YS, YS)
    token = local(mark_kernel, "mark", PARAMS, [(8, LANES)], after=strips[1:])
    (paired,) = local(pair_kernel, "pair", PARAMS, [own.shape], owner, own, far, after=token)
    last = swap(paired)
    left, right = split(linv, strips)
    top, swapped = ready(table, owner, own, got, far, window)
    return final(table, owner, left, right, swapped, top, give, last)


def solution(mesh):
    return jax.shard_map(
        functools.partial(on_device, mesh.shape["prow"], mesh.shape["pcol"]),
        mesh=mesh,
        in_specs=(P("prow", "pcol"), P(("prow", "pcol"), None), P(), P()),
        out_specs=P("prow", "pcol"),
        check_vma=False,
    )
```

```python
import functools

import jax
import jax.numpy as jnp
from jax import lax
from jax.experimental import pallas as pl
from jax.experimental.pallas import tpu as pltpu
from jax.sharding import PartitionSpec as P

CORES = 2
YS = 8
LANES = 128
STEP = 512
PARAMS = pltpu.CompilerParams(vmem_limit_bytes=32 * 1024 * 1024)
ROOMY = pltpu.CompilerParams(vmem_limit_bytes=58 * 1024 * 1024)


def vmem(count):
    return [pl.BlockSpec(memory_space=pltpu.VMEM)] * count


def smem(count):
    return [pl.BlockSpec(memory_space=pltpu.SMEM)] * count


def cost(flops, nbytes):
    return pl.CostEstimate(flops=flops, bytes_accessed=nbytes, transcendentals=0)


def tiles(ncols):
    return [slice(c, c + LANES) for c in range(0, ncols, LANES)]


def sides(half):
    me = lax.axis_index("prow")
    core = lax.rem(me, CORES)
    return me, me + 1 - 2 * core, core * half, half - core * half


def each(count, body):
    def four(j, carry):
        for u in range(4):
            body(jnp.minimum(4 * j + u, count - 1))
        return carry

    lax.fori_loop(0, (count + 3) // 4, four, 0)


def pick_kernel(piv, win, own, give, slots, rows, counts, held, sem):
    nrows = win.shape[0]
    half = own.shape[0]
    me, _, base, other = sides(half)
    first = me * nrows
    load = pltpu.make_async_copy(win, held, sem)
    load.start()

    def step(i, totals):
        new = []
        for side, start in enumerate((base, other)):
            local = piv[start + i] - first
            inside = (local >= 0) & (local < nrows)
            slots[side, totals[side]] = i
            rows[side, totals[side]] = local
            new.append(totals[side] + inside.astype(jnp.int32))
        return tuple(new)

    totals = lax.fori_loop(0, half, step, (jnp.int32(0), jnp.int32(0)), unroll=8)
    load.wait()
    for side, start, out in ((1, other, give), (0, base, own)):
        counts[side] = totals[side]
        out[...] = held[pl.ds(pl.multiple_of(start, half), half), :]

        def put(i, side=side, out=out):
            out[pl.ds(slots[side, i], 1), :] = held[pl.ds(rows[side, i], 1), :]

        each(totals[side], put)


def pick(pivots, window):
    half = pivots.shape[0] // CORES
    ncols = window.shape[1]
    block = jax.ShapeDtypeStruct((half, ncols), window.dtype)
    table = jax.ShapeDtypeStruct((CORES, half), jnp.int32)
    out = pl.pallas_call(
        pick_kernel,
        out_shape=(block, block, table, table, jax.ShapeDtypeStruct((CORES,), jnp.int32)),
        in_specs=smem(1) + [pl.BlockSpec(memory_space=pl.ANY)],
        out_specs=tuple(vmem(2) + smem(3)),
        scratch_shapes=[pltpu.VMEM(window.shape, window.dtype), pltpu.SemaphoreType.DMA],
        compiler_params=ROOMY,
        cost_estimate=cost(0, 16 * half * ncols),
        name="pick",
    )(pivots, window)
    return out[0], out[1], out[2:]


def half_of(owner, base, half):
    return owner[pl.ds(pl.multiple_of(base, half), half), :]


def deal_kernel(owner, own, got, panel, beside, out, rows):
    half, ncols = own.shape
    me, partner, base, _ = sides(half)
    who = half_of(owner, base, half)
    theirs = (who == partner) | ((who != me) & (who != jnp.where(me == 0, who, -1)))
    for cols in tiles(ncols):
        out[:, cols] = jnp.where(theirs, got[:, cols], own[:, cols])
    stack(1, panel, beside, rows)


def bit(weight):
    return lax.rem(lax.axis_index("pcol") // weight, 2)


def stack(weight, mine, theirs, out):
    count = mine.shape[0]
    for block, side in ((mine, bit(weight)), (theirs, 1 - bit(weight))):
        out[pl.ds(pl.multiple_of(side * count, count), count), :] = block[...]


def join_kernel(mine, theirs, out):
    stack(2, mine, theirs, out)


def ordered(index, pieces, put):
    count = pieces[0].shape[0]
    for d, piece in enumerate(pieces):
        source = lax.rem(index - d + len(pieces), len(pieces))
        put(pl.ds(pl.multiple_of(source * count, count), count), piece[...])


def home_kernel(nz, owner, got, mine, theirs, out, strip):
    half, ncols = got.shape
    part = half // nz
    me, _, base, _ = sides(half)
    at = pl.multiple_of(base + me // CORES * part, part)
    chip = owner[pl.ds(at, part), :] // CORES
    for cols in tiles(ncols):
        former = got[0:part, cols]
        top = former
        for z in range(1, nz):
            top = jnp.where(chip == z, got[z * part : (z + 1) * part, cols], top)
        for z in range(nz):
            out[z * part : (z + 1) * part, cols] = jnp.where(chip == z, former, top)

    stack(4, mine, theirs, strip)


def pair_kernel(owner, own, got, *refs):
    out = refs[-1]
    half, ncols = own.shape
    me, partner, base, _ = sides(half)
    who = half_of(owner, base, half)
    mine = (who == me) | (who == jnp.where(me == 0, partner, me))
    for cols in tiles(ncols):
        out[:, cols] = jnp.where(mine, own[:, cols], got[:, cols])


def local(kernel, name, params, shapes, *blocks, after=()):
    outs = tuple(jax.ShapeDtypeStruct(shape, jnp.float32) for shape in shapes)
    return pl.pallas_call(
        kernel,
        out_shape=outs,
        in_specs=vmem(len(blocks)) + [pl.BlockSpec(memory_space=pl.ANY)] * len(after),
        out_specs=tuple(vmem(len(outs))),
        compiler_params=params,
        cost_estimate=cost(0, 4 * sum(block.size for block in blocks)),
        name=name,
    )(*blocks, *after)


def parts(value):
    high = value.astype(jnp.bfloat16)
    return high, (value - high.astype(jnp.float32)).astype(jnp.bfloat16)


def split_kernel(linv, *refs):
    strips, (left, right) = refs[:-2], refs[-2:]
    nb = linv.shape[1]

    def put(value, out, rows):
        high, low = parts(value)
        out[rows, 0:nb] = high
        out[rows, nb : 2 * nb] = low
        out[rows, 2 * nb : 3 * nb] = high

    put(linv[...], left, slice(None))
    ordered(lax.axis_index("pcol") // YS, strips, lambda rows, value: put(value, right, rows))


def split(linv, strips):
    nb = linv.shape[1]
    nrows = sum(strip.shape[0] for strip in strips)
    return pl.pallas_call(
        split_kernel,
        out_shape=(
            jax.ShapeDtypeStruct((nb, 3 * nb), jnp.bfloat16),
            jax.ShapeDtypeStruct((nrows, 3 * nb), jnp.bfloat16),
        ),
        in_specs=vmem(1 + len(strips)),
        out_specs=tuple(vmem(2)),
        compiler_params=PARAMS,
        cost_estimate=cost(0, 10 * nb * (nb + nrows)),
        name="split",
    )(linv, *strips)


def ready_kernel(slots, rows, counts, owner, own, got, far, win, top, swapped):
    half, ncols = own.shape
    me, partner, base, other = sides(half)
    who = half_of(owner, base, half)
    for cols in tiles(ncols):
        theirs = jnp.where(who == partner, got[:, cols], far[:, cols])
        top[:, cols] = jnp.where(who == me, own[:, cols], theirs)
    swapped[...] = win[...]

    def put(source, side, start):
        def one(i):
            swapped[pl.ds(rows[side, i], 1), :] = source[pl.ds(start + slots[side, i], 1), :]

        each(counts[side], one)

    @pl.when(me == 0)
    def _():
        put(win, 0, base)
        put(win, 1, other)

    @pl.when(me == 1)
    def _():
        put(got, 0, 0)

    @pl.when(me > 1)
    def _():
        put(far, 0, 0)


def ready(table, owner, own, got, far, window):
    return pl.pallas_call(
        ready_kernel,
        out_shape=(
            jax.ShapeDtypeStruct(own.shape, own.dtype),
            jax.ShapeDtypeStruct(window.shape, window.dtype),
        ),
        in_specs=smem(3) + vmem(5),
        out_specs=tuple(vmem(2)),
        compiler_params=PARAMS,
        cost_estimate=cost(0, 8 * window.size + 16 * own.size),
        name="ready",
    )(*table, owner, own, got, far, window)


def final_kernel(slots, rows, counts, owner, left, right, swapped, top, give, got, out, full, rhs):
    half = top.shape[0]
    nb = 2 * half
    nrows, step = out.shape
    me, _, base, other = sides(half)
    base = pl.multiple_of(base, half)
    other = pl.multiple_of(other, half)
    at = pl.multiple_of(pl.program_id(0) * step, step)
    who = half_of(owner, other, half)
    full[pl.ds(base, half), :] = top[:, pl.ds(at, step)]
    for c in range(0, step, LANES):
        cols = pl.ds(pl.multiple_of(at + c, LANES), LANES)
        full[pl.ds(other, half), c : c + LANES] = jnp.where(who == me, give[:, cols], got[:, cols])

    def product(factor, value):
        high, low = parts(value)
        rhs[0:nb, :] = high
        rhs[nb : 2 * nb, :] = high
        rhs[2 * nb : 3 * nb, :] = low
        return jnp.dot(factor[...], rhs[...], preferred_element_type=jnp.float32)

    out[...] = swapped[:, pl.ds(at, step)]

    def put(i):
        out[pl.ds(rows[1, i], 1), :] = got[pl.ds(slots[1, i], 1), pl.ds(at, step)]

    each(jnp.where(me == 0, 0, counts[1]), put)
    solved = product(left, full[...])
    out[...] = out[...] - product(right, solved)

    @pl.when(me == 0)
    def _():
        out[0:nb, :] = solved


def final(table, owner, left, right, swapped, top, give, got):
    nrows, ncols = swapped.shape
    nb = 2 * top.shape[0]
    step = min(STEP, ncols)
    return pl.pallas_call(
        final_kernel,
        grid=(ncols // step,),
        out_shape=jax.ShapeDtypeStruct(swapped.shape, swapped.dtype),
        in_specs=smem(3) + vmem(7),
        out_specs=pl.BlockSpec((nrows, step), lambda c: (0, c)),
        scratch_shapes=[pltpu.VMEM((nb, step), jnp.float32), pltpu.VMEM((3 * nb, step), jnp.bfloat16)],
        compiler_params=PARAMS,
        cost_estimate=cost(6 * (nb + nrows) * nb * ncols, 8 * nrows * ncols),
        name="final",
    )(*table, owner, left, right, swapped, top, give, got)


def on_device(nprow, npcol, window, panel, linv, pivots):
    nrows, ncols = window.shape
    nbw = pivots.shape[0]
    nz = nprow // CORES
    columns = [[z * CORES + core for z in range(nz)] for core in range(CORES)]

    def swap(value):
        return lax.ppermute(value, "prow", [(p, p ^ 1) for p in range(nprow)])

    def exchange(value):
        return lax.all_to_all(value, "prow", 0, 0, axis_index_groups=columns, tiled=True)

    def across(value, weight):
        return lax.ppermute(value, "pcol", [(c, c ^ weight) for c in range(npcol)])

    def ring(value, size, stride):
        span = size * stride
        pairs = lambda d: [(c, c // span * span + (c + d * stride) % span) for c in range(npcol)]
        return [value] + [lax.ppermute(value, "pcol", pairs(d)) for d in range(1, size)]

    owner = jnp.broadcast_to((pivots // nrows)[:, None], (nbw, LANES))
    count = panel.shape[0]

    own, give, table = pick(pivots, window)
    got = swap(give)
    beside = across(panel, 1)
    chip, rows = local(deal_kernel, "deal", PARAMS, [own.shape, (2 * count, nbw)], owner, own, got, panel, beside)
    dealt = exchange(chip)
    (mine,) = local(join_kernel, "join", PARAMS, [(4 * count, nbw)], rows, across(rows, 2))
    kernel, shapes = functools.partial(home_kernel, nz), [own.shape, (YS * count, nbw)]
    chosen, strip = local(kernel, "home", ROOMY, shapes, owner, dealt, mine, across(mine, 4))
    far = exchange(chosen)
    strips = ring(strip, npcol // YS, YS)
    (paired,) = local(pair_kernel, "pair", PARAMS, [own.shape], owner, own, far, after=strips[1:])
    last = swap(paired)
    left, right = split(linv, strips)
    top, swapped = ready(table, owner, own, got, far, window)
    return final(table, owner, left, right, swapped, top, give, last)


def solution(mesh):
    return jax.shard_map(
        functools.partial(on_device, mesh.shape["prow"], mesh.shape["pcol"]),
        mesh=mesh,
        in_specs=(P("prow", "pcol"), P(("prow", "pcol"), None), P(), P()),
        out_specs=P("prow", "pcol"),
        check_vma=False,
    )
```
